32 devices in a mesh: rep: 4 (over z), dom: 8 (over y, x, core).
Axes of the slice: x: 2, y: 2, z: 4, core: 2. Of those that a mesh axis runs over, the one named last changes fastest.
Arguments:
- feats: bfloat16 [12288, 256], P(('rep', 'dom')), may hold values from -6 to 6
- cotangent: bfloat16 [12288, 256], P(('rep', 'dom')), may hold values from -6 to 6
- weight: bfloat16 [256, 256], replicated, may hold values from -0.375 to 0.375
- bias: float32 [256], replicated, may hold values from -3 to 3
- in_vals: bfloat16 [96, 4, 2, 128, 128], P(('rep', 'dom')), may hold values from -0.125 to 0.125
- in_cols: int32 [96, 4, 2], P(('rep', 'dom')), may hold values from 0 to 2, as said below
- off_vals: bfloat16 [96, 9, 128, 128], P(('rep', 'dom')), may hold values from -0.125 to 0.125
- off_ref: int32 [96, 9], P(('rep', 'dom')), may hold values from 0 to 7, as said below
- want: int32 [4, 8, 8, 1], P('rep', 'dom'), may hold values from 0 to 2, as said below
Outputs:
- activated: bfloat16 [12288, 256], P(('rep', 'dom'))
- grad_feats: bfloat16 [12288, 256], P(('rep', 'dom'))
- grad_weight: bfloat16 [256, 256], replicated
The draws below stay inside these ranges and needn't reach their ends.
Inputs may be any that keep to these rules, and one draw needn't show every extreme that they name: in_cols[b, s, k] is a block of panel (s, e) of the row block's own domain e; the 2 entries in_cols[b, s, :] differ. want[q, e, f, c] is a block, numbered within panel (q, f), that panel (q, e) asks of panel (q, f); the 1 entries of one request differ. off_ref[b, k] = f + c names block want[q, e, f, c] for a row block b of panel (q, e); f is never e. For each cycle position q some domain f has all its 1 slots named by the tiles of every panel (q, e) with e other than f.
All inputs are finite; a program needn't handle non-finite values.
Results may differ from the reference program's by a relative error of at most 0.009.
Values may be sent and summed in bfloat16 or wider, within the bound.
No kernel may reach another device: no remote copies, remote signals or barrier semaphores. Data moves between devices by JAX's collectives and lax.ppermute only.
A program may use at most 128 MiB of HBM per device.

```python
import math
import jax
import jax.numpy as jnp
from jax import lax

HID = 256
BLK = 128
NODE_DEV = 384
KP = 2
KOFF = 9
CAP = 1
CYCLE = 4
DOMS = 8
NODES = 12288


def routing_tables(key):
    key = jax.random.fold_in(key, 7)
    devices = CYCLE * DOMS
    blocks = NODE_DEV // BLK
    tile_count = blocks * KOFF
    slot_count = DOMS * CAP
    keys = jax.random.split(key, 6)
    hot_owner = jax.random.randint(keys[0], (CYCLE,), 0, DOMS)
    cycle_of = jnp.arange(devices) // DOMS
    domain_of = jnp.arange(devices) % DOMS
    hot_device = hot_owner[cycle_of]
    block_scores = jax.random.randint(keys[1], (devices, DOMS, blocks), 0, 1 << 20) * blocks + jnp.arange(blocks)
    asked = jnp.argsort(block_scores, axis=-1)[..., :CAP]
    slot_owner = jnp.arange(slot_count) // CAP
    is_self = slot_owner[None, :] == domain_of[:, None]
    is_hot = (slot_owner[None, :] == hot_device[:, None]) & jnp.logical_not(is_self)
    ranking = jnp.where(is_hot, 0, jnp.where(is_self, 2, 1))
    slot_scores = (ranking * (1 << 20) + jax.random.randint(keys[2], (devices, slot_count), 0, 1 << 20)) * slot_count + jnp.arange(slot_count)
    slot_order = jnp.argsort(slot_scores, axis=-1)
    top_most = min(tile_count - CAP, (DOMS - 2) * CAP)
    spread_draw = jax.random.randint(keys[3], (devices,), 0, max(top_most // 2, 1))
    extra = top_most - spread_draw * spread_draw // top_most
    live = jnp.where(hot_device == domain_of, 0, CAP) + extra
    tile_ids = jnp.arange(tile_count)
    filler = jax.random.randint(keys[4], (devices, tile_count), 0, 1 << 20) % live[:, None]
    position = jnp.where(tile_ids[None, :] < live[:, None], tile_ids[None, :], filler)
    refs = jnp.take_along_axis(slot_order, position, axis=-1)
    shuffle = jnp.argsort(jax.random.randint(keys[5], (devices, tile_count), 0, 1 << 20) * tile_count + tile_ids, axis=-1)
    refs = jnp.take_along_axis(refs, shuffle, axis=-1)
    want_table = asked.astype(jnp.int32).reshape(CYCLE, DOMS, DOMS, CAP)
    ref_table = refs.astype(jnp.int32).reshape(devices * blocks, KOFF)
    return (want_table, ref_table)


def draw_want(key, part):
    return routing_tables(key)[0]


def draw_off_ref(key, part):
    return routing_tables(key)[1]


def draw_in_cols(key, part):
    key = jax.random.fold_in(key, 3)
    blocks = NODE_DEV // BLK
    row_count = NODES // BLK * CYCLE
    scores = jax.random.randint(key, (row_count, blocks), 0, 1 << 20) * blocks + jnp.arange(blocks)
    order = jnp.argsort(scores, axis=-1)[:, :KP]
    return order.astype(jnp.int32).reshape(NODES // BLK, CYCLE, KP)


def block_scale(rng, extent, cuts, low, top_value):
    level, own = 1.0, jax.random.fold_in(rng, 6)
    for dim, parts in cuts:
        draws = jnp.exp(jax.random.uniform(jax.random.fold_in(own, dim), (parts,), jnp.float32, low / len(cuts), top_value / len(cuts)))
        level = level * jnp.repeat(draws, extent[dim] // parts).reshape([-1 if axis == dim else 1 for axis in range(len(extent))])
    return level


def scatter_about(own_key, extent, scale, limit, pieces=(), dtype=jnp.bfloat16):
    factor_of = block_scale(own_key, extent, pieces, -0.22, 0.18) if pieces else 1.0
    entries = jax.random.normal(own_key, extent, jnp.float32) * scale * factor_of
    return jnp.minimum(jnp.maximum(entries, -limit), limit).astype(dtype)


def setup_inputs(seed: int = 0) -> dict:
    streams_of = jax.random.split(jax.random.key(seed), 10)
    feats = scatter_about(streams_of[0], (NODES, HID), 1.0, 6.0, ((0, 32),))
    cotangent = scatter_about(streams_of[1], (NODES, HID), 1.0, 6.0, ((0, 32),))
    weight = scatter_about(streams_of[2], (HID, HID), HID ** -0.5, 0.375)
    bias = scatter_about(streams_of[3], (HID,), 0.5, 3.0, (), jnp.float32)
    in_vals = scatter_about(streams_of[4], (NODES // BLK, CYCLE, KP, BLK, BLK), (BLK * (CYCLE * KP + KOFF)) ** -0.5, 0.125, ((0, 32),))
    in_cols = draw_in_cols(jax.random.fold_in(streams_of[9], 71), 0)
    off_vals = scatter_about(streams_of[6], (NODES // BLK, KOFF, BLK, BLK), (BLK * (CYCLE * KP + KOFF)) ** -0.5, 0.125, ((0, 32),))
    off_ref = draw_off_ref(jax.random.fold_in(streams_of[9], 71), 0)
    want = draw_want(jax.random.fold_in(streams_of[9], 71), 0)
    return dict(feats=feats, cotangent=cotangent, weight=weight, bias=bias, in_vals=in_vals, in_cols=in_cols, off_vals=off_vals, off_ref=off_ref, want=want)


def rounded(values):
    return lax.optimization_barrier(values.astype(jnp.bfloat16)).astype(jnp.float32)

def reference(feats, cotangent, weight, bias, in_vals, in_cols, off_vals, off_ref, want):
    blocks = NODE_DEV // BLK
    slot_count = DOMS * CAP
    devices = CYCLE * DOMS
    feat_blocks = feats.reshape(CYCLE, DOMS, blocks, BLK, HID)
    dev_vals = in_vals.reshape(devices, blocks, CYCLE, KP, BLK, BLK)
    dev_cols = in_cols.reshape(devices, blocks, CYCLE, KP)
    dev_off = off_vals.reshape(devices, blocks, KOFF, BLK, BLK)
    dev_ref = off_ref.reshape(devices, blocks, KOFF)
    dev_want = want.reshape(devices, DOMS, CAP)
    cycle_ids = (jnp.arange(devices) // DOMS).astype(jnp.int32)
    domain_ids = (jnp.arange(devices) % DOMS).astype(jnp.int32)
    cycle_range = jnp.arange(CYCLE).astype(jnp.int32)
    domain_range = jnp.arange(DOMS).astype(jnp.int32)
    block_range = jnp.arange(blocks).astype(jnp.int32)

    def aggregate_one(pack):
        tile_set, columns, off_tiles, refs, asked, cycle_id, domain_id = pack
        domain_rows = jnp.take(feat_blocks, domain_id, axis=1)
        picked = domain_rows[cycle_range[None, :, None], columns]
        inner_part = jnp.einsum('iskab,iskbf->iaf', tile_set.astype(jnp.float32), picked.astype(jnp.float32))
        same_cycle = jnp.take(feat_blocks, cycle_id, axis=0)
        fetched = same_cycle[domain_range[:, None], asked].reshape(slot_count, BLK, HID)
        outer_part = jnp.einsum('ikab,ikbf->iaf', off_tiles.astype(jnp.float32), fetched[refs].astype(jnp.float32))
        return (inner_part + outer_part).astype(jnp.bfloat16)
    aggregate = lax.map(aggregate_one, (dev_vals, dev_cols, dev_off, dev_ref, dev_want, cycle_ids, domain_ids))
    aggregate = aggregate.reshape(NODES, HID)
    pre_act = jnp.dot(aggregate, weight, preferred_element_type=jnp.float32) + bias
    activated = jax.nn.gelu(pre_act).astype(jnp.bfloat16)
    _, pullback = jax.vjp(jax.nn.gelu, pre_act)
    grad_pre = pullback(cotangent.astype(jnp.float32))[0].astype(jnp.bfloat16)
    grad_weight = jnp.dot(aggregate.T, grad_pre, preferred_element_type=jnp.float32)
    grad_weight = (grad_weight * (1.0 / math.sqrt(NODES))).astype(jnp.bfloat16)
    grad_agg = jnp.dot(grad_pre, weight.T, preferred_element_type=jnp.float32).astype(jnp.bfloat16)
    grad_blocks = grad_agg.reshape(CYCLE, DOMS, blocks, BLK, HID)

    def inner_terms(tile_set, columns, grads):
        spread = jnp.einsum('iskab,iaf->iskbf', tile_set.astype(jnp.float32), grads.astype(jnp.float32))
        onehot = (columns[..., None] == block_range).astype(jnp.float32)
        term_rows = jnp.einsum('iskj,iskbf->sjbf', onehot, spread, precision=lax.Precision.HIGHEST)
        return rounded(term_rows)

    def inner_step(summed, pack):
        tile_set, columns, grads = pack
        return (summed + jax.vmap(inner_terms)(tile_set, columns, grads), None)
    vals_grid = in_vals.reshape(CYCLE, DOMS, blocks, CYCLE, KP, BLK, BLK)
    cols_grid = in_cols.reshape(CYCLE, DOMS, blocks, CYCLE, KP)
    inner_start = jnp.zeros((DOMS, CYCLE, blocks, BLK, HID), jnp.float32)
    inner_sum = lax.scan(inner_step, inner_start, (vals_grid, cols_grid, grad_blocks))[0]
    inner_grad = jnp.transpose(inner_sum, (1, 0, 2, 3, 4))

    def outer_terms(off_tiles, refs, asked, grads):
        spread = jnp.einsum('ikab,iaf->ikbf', off_tiles.astype(jnp.float32), grads.astype(jnp.float32))
        summed = jax.ops.segment_sum(spread.reshape(blocks * KOFF, BLK, HID), refs.reshape(blocks * KOFF), num_segments=slot_count)
        summed = rounded(summed).reshape(DOMS, CAP, BLK, HID)
        onehot = (asked[..., None] == block_range).astype(jnp.float32)
        return jnp.einsum('ocj,ocbf->ojbf', onehot, summed, precision=lax.Precision.HIGHEST)

    def outer_step(summed, pack):
        off_tiles, refs, asked, grads = pack
        return (summed + jax.vmap(outer_terms)(off_tiles, refs, asked, grads), None)
    off_grid = jnp.swapaxes(off_vals.reshape(CYCLE, DOMS, blocks, KOFF, BLK, BLK), 0, 1)
    ref_grid = jnp.swapaxes(off_ref.reshape(CYCLE, DOMS, blocks, KOFF), 0, 1)
    want_grid = jnp.swapaxes(want, 0, 1)
    grad_grid = jnp.swapaxes(grad_blocks, 0, 1)
    outer_start = jnp.zeros((CYCLE, DOMS, blocks, BLK, HID), jnp.float32)
    outer_grad = lax.scan(outer_step, outer_start, (off_grid, ref_grid, want_grid, grad_grid))[0]
    grad_feats = (inner_grad + outer_grad).astype(jnp.bfloat16).reshape(NODES, HID)
    return (activated, grad_feats, grad_weight)
```

```python
import functools
import math

import jax
import jax.numpy as jnp
from jax import lax
from jax.experimental import pallas as pl
from jax.experimental.pallas import tpu as pltpu
from jax.sharding import PartitionSpec as P

F32, BF16 = jnp.float32, jnp.bfloat16
ROOT = math.sqrt(2.0 / math.pi)
CUBIC = 0.044715


def partners(count):
    if count & (count - 1) == 0:
        return [[(i, i ^ k) for i in range(count)] for k in range(1, count)]
    return [[(i, (i + k) % count) for i in range(count)] for k in range(1, count)]


def source_of(me, k, count):
    return me ^ k if count & (count - 1) == 0 else (me - k + count) % count


def call(body, outs, args, kinds, scratch=(), flops=0, name=None):
    spaces = {"s": pltpu.SMEM, "v": pltpu.VMEM}
    nbytes = sum(math.prod(a.shape) * a.dtype.itemsize for a in (*args, *outs))
    work = sum(math.prod(s.shape) * jnp.dtype(s.dtype).itemsize for s in scratch)
    return pl.pallas_call(
        body,
        out_shape=outs,
        in_specs=[pl.BlockSpec(memory_space=spaces[k]) for k in kinds],
        out_specs=[pl.BlockSpec(memory_space=pltpu.VMEM) for _ in outs],
        scratch_shapes=list(scratch),
        cost_estimate=pl.CostEstimate(flops=flops, bytes_accessed=nbytes, transcendentals=0),
        compiler_params=pltpu.CompilerParams(vmem_limit_bytes=nbytes + work + (8 << 20)),
        name=name,
    )(*args)


def arrange(count, order_ref, cols_ref, in_ref, off_ref, a_ref, at_ref, offt_ref):
    blocks, _, pairs, edge, _ = in_ref.shape
    rows = blocks * edge
    a_ref[...] = jnp.zeros_like(a_ref)
    at_ref[...] = jnp.zeros_like(at_ref)
    for n in range(count):
        s = order_ref[n]
        for b in range(blocks):
            for k in range(pairs):
                tile = in_ref[b, s, k]
                start = pl.multiple_of(n * rows + cols_ref[b, s, k] * edge, edge)
                a_ref[b * edge:(b + 1) * edge, pl.ds(start, edge)] = tile
                at_ref[pl.ds(start, edge), b * edge:(b + 1) * edge] = tile.T
    for b in range(blocks):
        for k in range(off_ref.shape[1]):
            offt_ref[b, k] = off_ref[b, k].T


def pick(edge, served_ref, panel_ref, out_ref):
    for slot in range(out_ref.shape[0]):
        out_ref[slot] = panel_ref[pl.ds(pl.multiple_of(served_ref[slot] * edge, edge), edge), :]


def layer(count, refs_ref, *args):
    panels = args[:count]
    (a_ref, off_ref, block_ref, weight_ref, bias_ref, cot_ref,
     act_ref, agg_ref, pre_ref, grad_ref) = args[count:]
    blocks, tiles, edge, _ = off_ref.shape
    rows = blocks * edge
    for b in range(blocks):
        part = slice(b * edge, (b + 1) * edge)
        total = jnp.zeros((edge, weight_ref.shape[0]), F32)
        for n in range(count):
            total += jnp.dot(a_ref[part, n * rows:(n + 1) * rows], panels[n][...], preferred_element_type=F32)
        for k in range(0, tiles, 2):
            ks = range(k, min(k + 2, tiles))
            left = jnp.concatenate([off_ref[b, i] for i in ks], axis=1)
            right = jnp.concatenate([block_ref[refs_ref[b, i]] for i in ks], axis=0)
            total += jnp.dot(left, right, preferred_element_type=F32)
        agg = total.astype(BF16)
        agg_ref[part, :] = agg
        v = jnp.dot(agg, weight_ref[...], preferred_element_type=F32) + bias_ref[...]
        t = jnp.tanh(ROOT * (v + CUBIC * (v * v * v)))
        act_ref[part, :] = (0.5 * v * (1.0 + t)).astype(BF16)
        slope = 0.5 * (1.0 + t) + 0.5 * v * (1.0 - t * t) * (ROOT * (1.0 + 3.0 * CUBIC * (v * v)))
        grad = (cot_ref[part, :].astype(F32) * slope).astype(BF16)
        pre_ref[part, :] = grad
        grad_ref[part, :] = lax.dot_general(
            grad, weight_ref[...], (((1,), (1,)), ((), ())), preferred_element_type=F32).astype(BF16)


def spread_inner(count, at_ref, grad_ref, *outs):
    rows = grad_ref.shape[0]
    for n in range(count):
        outs[n][...] = jnp.dot(at_ref[n * rows:(n + 1) * rows, :], grad_ref[...], preferred_element_type=F32).astype(BF16)


def spread_outer(refs_ref, offt_ref, grad_ref, agg_ref, pre_ref, out_ref, total_ref):
    blocks, tiles, edge, _ = offt_ref.shape
    slots, width = total_ref.shape[0], total_ref.shape[2]
    total_ref[...] = jnp.zeros_like(total_ref)
    for b in range(blocks):
        grad = grad_ref[b * edge:(b + 1) * edge, :]
        for k in range(tiles):
            slot = refs_ref[b, k]
            total_ref[slot] += jnp.dot(offt_ref[b, k], grad, preferred_element_type=F32)
    out_ref[:, :edge, :] = total_ref[...].astype(BF16)
    term = lax.dot_general(agg_ref[...], pre_ref[...], (((0,), (0,)), ((), ())), preferred_element_type=F32)
    out_ref[:, edge:, :] = term.astype(BF16).reshape(slots, width // slots, width)


def finish_weight(edge, coming_ref, out_ref):
    out_ref[...] = jnp.sum(coming_ref[:, edge:, :].astype(F32), axis=0).astype(BF16)


def finish(edge, served_ref, coming_ref, *args):
    terms, out_ref, total_ref = args[:-2], args[-2], args[-1]
    total = terms[0][...].astype(F32)
    for t in terms[1:]:
        total += t[...].astype(F32)
    total_ref[...] = total
    for slot in range(coming_ref.shape[0]):
        part = pl.ds(pl.multiple_of(served_ref[slot] * edge, edge), edge)
        total_ref[part, :] += coming_ref[slot, :edge, :].astype(F32)
    out_ref[...] = total_ref[...].astype(BF16)


def local(feats, cotangent, weight, bias, in_vals, in_cols, off_vals, off_ref, want):
    count, doms = lax.axis_size("rep"), lax.axis_size("dom")
    me = lax.axis_index("rep")
    blocks, _, _, edge, _ = in_vals.shape
    rows, width = feats.shape
    requests = want.reshape(want.shape[2], want.shape[3])
    slots = requests.size
    share = width // slots
    shape = jax.ShapeDtypeStruct
    perms = partners(count)

    panels = [feats] + [lax.ppermute(feats, "rep", p) for p in perms]
    order = jnp.stack([source_of(me, k, count) for k in range(count)]).astype(jnp.int32)
    served = lax.all_to_all(requests, "dom", split_axis=0, concat_axis=0, tiled=True).reshape(slots)
    picked = call(functools.partial(pick, edge), [shape((slots, edge, width), BF16)], (served, feats), "sv", name="pick")[0]
    arrived = lax.all_to_all(picked, "dom", split_axis=0, concat_axis=0, tiled=True)

    a, at, offt = call(
        functools.partial(arrange, count),
        [shape((rows, count * rows), BF16), shape((count * rows, rows), BF16), shape(off_vals.shape, BF16)],
        (order, in_cols, in_vals, off_vals), "ssvv", name="arrange")
    flat = shape((rows, width), BF16)
    activated, agg, grad_pre, grad_agg = call(
        functools.partial(layer, count), [flat] * 4,
        (off_ref, *panels, a, off_vals, arrived, weight, bias.reshape(1, width), cotangent),
        "s" + "v" * (count + 6), flops=10**9, name="layer")
    terms = call(functools.partial(spread_inner, count), [flat] * count, (at, grad_agg), "vv", flops=10**9, name="inner")
    got = [terms[0]] + [lax.ppermute(t, "rep", [(b, a) for a, b in p]) for t, p in zip(terms[1:], perms)]
    outer = call(
        spread_outer, [shape((slots, edge + share, width), BF16)], (off_ref, offt, grad_agg, agg, grad_pre), "svvvv",
        scratch=[pltpu.VMEM((slots, edge, width), F32)], flops=10**9, name="outer")[0]
    coming = lax.all_to_all(outer, "dom", split_axis=0, concat_axis=0, tiled=True)
    mine = call(functools.partial(finish_weight, edge), [shape((share, width), BF16)], (coming,), "v", name="weight")[0]
    shares = [mine] + [lax.ppermute(mine, "rep", p) for p in perms]
    scale = 1.0 / math.sqrt(rows * count * doms)
    whole = (sum(s.astype(F32) for s in shares) * scale).astype(BF16)
    grad_weight = lax.all_gather(whole, "dom", axis=0, tiled=True)
    grad_feats = call(
        functools.partial(finish, edge), [flat], (served, coming, *got), "sv" + "v" * count,
        scratch=[pltpu.VMEM((rows, width), F32)], name="finish")[0]
    return (activated, grad_feats, grad_weight)


def solution(mesh):
    in_specs = (
        P(("rep", "dom"), None),
        P(("rep", "dom"), None),
        P(),
        P(),
        P(("rep", "dom"), None, None, None, None),
        P(("rep", "dom"), None, None),
        P(("rep", "dom"), None, None, None),
        P(("rep", "dom"), None),
        P("rep", "dom", None, None),
    )
    out_specs = (P(("rep", "dom"), None), P(("rep", "dom"), None), P())
    return jax.shard_map(local, mesh=mesh, in_specs=in_specs, out_specs=out_specs, check_vma=False)
```

```python
import functools
import math

import jax
import jax.numpy as jnp
from jax import lax
from jax.experimental import pallas as pl
from jax.experimental.pallas import tpu as pltpu
from jax.sharding import PartitionSpec as P

F32, BF16 = jnp.float32, jnp.bfloat16
ROOT = math.sqrt(2.0 / math.pi)
CUBIC = 0.044715


def swapped(value, axis, k):
    return lax.ppermute(value, axis, [(i, i ^ k) for i in range(lax.axis_size(axis))])


def after(value, other):
    return value if other is None else lax.optimization_barrier((value, other))[0]


def fenced(sure, body, *args):
    blank = lambda *args: jax.tree.map(lambda s: jnp.zeros(s.shape, s.dtype), jax.eval_shape(body, *args))
    return lax.cond(sure, body, blank, *args)


def call(body, outs, args, kinds, scratch=(), flops=0, name=None):
    spaces = {"s": pltpu.SMEM, "v": pltpu.VMEM, "h": pltpu.HBM}
    nbytes = sum(math.prod(a.shape) * a.dtype.itemsize for a in (*args, *outs))
    work = sum(math.prod(s.shape) * jnp.dtype(s.dtype).itemsize for s in scratch if s.memory_space == pltpu.VMEM)
    return pl.pallas_call(
        body,
        out_shape=outs,
        in_specs=[pl.BlockSpec(memory_space=spaces[k]) for k in kinds],
        out_specs=[pl.BlockSpec(memory_space=pltpu.VMEM) for _ in outs],
        scratch_shapes=list(scratch),
        cost_estimate=pl.CostEstimate(flops=flops, bytes_accessed=nbytes, transcendentals=0),
        compiler_params=pltpu.CompilerParams(vmem_limit_bytes=nbytes + work + (4 << 20)),
        name=name,
    )(*args)


def arrange(count, me_ref, cols_ref, in_hbm, off_hbm, a_ref, at_ref, offt_ref, in_ref, off_ref, in_sem, off_sem):
    blocks, _, pairs, edge, _ = in_ref.shape
    rows = blocks * edge
    in_copies = [pltpu.make_async_copy(in_hbm.at[b], in_ref.at[b], in_sem.at[b]) for b in range(blocks)]
    off_copies = [pltpu.make_async_copy(off_hbm.at[b], off_ref.at[b], off_sem.at[b]) for b in range(blocks)]
    for copy in in_copies + off_copies:
        copy.start()
    a_ref[...] = jnp.zeros_like(a_ref)
    at_ref[...] = jnp.zeros_like(at_ref)
    for b in range(blocks):
        in_copies[b].wait()
        for n in range(count):
            s = me_ref[0] ^ n
            for k in range(pairs):
                tile = in_ref[b, s, k]
                start = pl.multiple_of(n * rows + cols_ref[b, k, s] * edge, edge)
                a_ref[b * edge:(b + 1) * edge, pl.ds(start, edge)] = tile
                at_ref[pl.ds(start, edge), b * edge:(b + 1) * edge] = tile.T
    for b in range(blocks):
        off_copies[b].wait()
        for k in range(off_ref.shape[1]):
            offt_ref[b, k] = off_ref[b, k].T


def layer(count, doms, me_ref, want_ref, refs_ref, *args):
    panels, others = args[:count], args[count:count + doms - 1]
    (a_ref, at_ref, off_ref, weight_ref, bias_ref, cot_ref,
     act_ref, grad_ref, term_ref, *outs, agg_ref, pre_ref, block_ref) = args[count + doms - 1:]
    blocks, tiles, edge, _ = off_ref.shape
    rows, cap = blocks * edge, want_ref.shape[0]
    for n in range(1, doms):
        f = me_ref[1] ^ n
        for c in range(cap):
            block_ref[f * cap + c] = others[n - 1][pl.ds(pl.multiple_of(want_ref[c, f] * edge, edge), edge), :]
    for b in range(blocks):
        part = slice(b * edge, (b + 1) * edge)
        total = jnp.zeros((edge, weight_ref.shape[0]), F32)
        for n in range(count):
            total += jnp.dot(a_ref[part, n * rows:(n + 1) * rows], panels[n][...], preferred_element_type=F32)
        for k in range(0, tiles, 2):
            ks = range(k, min(k + 2, tiles))
            left = jnp.concatenate([off_ref[b, i] for i in ks], axis=1)
            right = jnp.concatenate([block_ref[refs_ref[b, i]] for i in ks], axis=0)
            total += jnp.dot(left, right, preferred_element_type=F32)
        agg = total.astype(BF16)
        agg_ref[part, :] = agg
        v = jnp.dot(agg, weight_ref[...], preferred_element_type=F32) + bias_ref[...]
        t = jnp.tanh(ROOT * (v + CUBIC * (v * v * v)))
        act_ref[part, :] = (0.5 * v * (1.0 + t)).astype(BF16)
        slope = 0.5 * (1.0 + t) + 0.5 * v * (1.0 - t * t) * (ROOT * (1.0 + 3.0 * CUBIC * (v * v)))
        grad = (cot_ref[part, :].astype(F32) * slope).astype(BF16)
        pre_ref[part, :] = grad
        grad_ref[part, :] = lax.dot_general(
            grad, weight_ref[...], (((1,), (1,)), ((), ())), preferred_element_type=F32).astype(BF16)

    term_ref[...] = lax.dot_general(
        agg_ref[...], pre_ref[...], (((0,), (0,)), ((), ())), preferred_element_type=F32).astype(BF16)
    for n in range(count):
        outs[n][...] = jnp.dot(at_ref[n * rows:(n + 1) * rows, :], grad_ref[...], preferred_element_type=F32).astype(BF16)


def spread_outer(want_ref, refs_ref, offt_ref, grad_ref, out_ref, total_ref):
    blocks, tiles, edge, _ = offt_ref.shape
    cap, doms = want_ref.shape
    total_ref[...] = jnp.zeros_like(total_ref)
    for b in range(blocks):
        grad = grad_ref[b * edge:(b + 1) * edge, :]
        for k in range(tiles):
            total_ref[refs_ref[b, k]] += jnp.dot(offt_ref[b, k], grad, preferred_element_type=F32)
    for f in range(doms):
        for c in range(cap):
            out_ref[f, c * edge:(c + 1) * edge, :] = total_ref[f * cap + c].astype(BF16)
            top = cap * edge + c * 16
            out_ref[f, top:top + 16, :] = jnp.full((16, out_ref.shape[2]), want_ref[c, f], jnp.int32).astype(BF16)


def joined(part, axis, k):
    return (part.astype(F32) + swapped(part, axis, k).astype(F32)).astype(BF16)


def finish(cap, edge, coming_ref, *args):
    terms, out_ref = args[:-1], args[-1]
    for j in range(out_ref.shape[0] // edge):
        part = slice(j * edge, (j + 1) * edge)
        total = terms[0][part, :].astype(F32)
        for ref in terms[1:]:
            total += ref[part, :].astype(F32)
        for f in range(coming_ref.shape[0]):
            for c in range(cap):
                top = cap * edge + c * 16
                place = coming_ref[f, top:top + 1, :].astype(F32)
                total += jnp.where(place == j, coming_ref[f, c * edge:(c + 1) * edge, :].astype(F32), 0.0)
        out_ref[part, :] = total.astype(BF16)


def local(feats, cotangent, weight, bias, in_vals, in_cols, off_vals, off_ref, want):
    count, doms = lax.axis_size("rep"), lax.axis_size("dom")
    me = jnp.stack([lax.axis_index("rep"), lax.axis_index("dom")]).astype(jnp.int32)
    blocks, _, _, edge, _ = in_vals.shape
    rows, width = feats.shape
    requests = want.transpose(0, 1, 3, 2).reshape(want.shape[3], want.shape[2])
    cap = requests.shape[0]
    share = width // doms
    shape = jax.ShapeDtypeStruct
    flat = shape((rows, width), BF16)

    slots = doms * cap
    piece = shape((share, width), BF16)
    sure = requests[0, 0] >= 0
    scale = 1.0 / math.sqrt(rows * count * doms)

    def exchange(outer, term):
        coming = lax.all_to_all(outer, "dom", split_axis=0, concat_axis=0, tiled=True)
        k = 1
        while k < doms:
            term, k = joined(term, "dom", k), 2 * k
        k = 1
        while 2 * k < count:
            term, k = joined(term, "rep", k), 2 * k
        return coming, term

    panels = [feats] + [swapped(feats, "rep", k) for k in range(1, count)]
    even = [feats] + [swapped(feats, "dom", k) for k in range(2, doms, 2)]
    dma = pltpu.SemaphoreType.DMA((blocks,))
    a, at, offt = call(
        functools.partial(arrange, count),
        [shape((rows, count * rows), BF16), shape((count * rows, rows), BF16), shape(off_vals.shape, BF16)],
        (after(me, even[2]), in_cols.transpose(0, 2, 1), in_vals, off_vals), "sshh",
        scratch=[pltpu.VMEM(in_vals.shape, BF16), pltpu.VMEM(off_vals.shape, BF16), dma, dma], name="arrange")
    odd = [swapped(after(value, offt), "dom", 1) for value in even]
    others = [value for pair in zip(even, odd) for value in pair][1:]
    activated, grad_agg, term, *terms = call(
        functools.partial(layer, count, doms), [flat] * 2 + [shape((width, width), BF16)] + [flat] * count,
        (me, requests, off_ref, *panels, *others, a, at, off_vals, weight, bias.reshape(1, width), cotangent),
        "sss" + "v" * (count + doms + 5),
        scratch=[pltpu.VMEM((rows, width), BF16)] * 2 + [pltpu.VMEM((slots, edge, width), BF16)],
        flops=10**9, name="layer")
    got = [terms[0]] + [swapped(terms[k], "rep", k) for k in range(1, count)]
    outer = call(
        spread_outer, [shape((doms, cap * (edge + 16), width), BF16)], (requests, off_ref, offt, grad_agg), "ssvv",
        scratch=[pltpu.VMEM((slots, edge, width), F32)], flops=10**9, name="outer")[0]
    coming, term = fenced(sure, exchange, outer, term)
    term, *got = lax.optimization_barrier((term, *got))
    grad_weight = ((term.astype(F32) + swapped(term, "rep", count // 2).astype(F32)) * scale).astype(BF16)
    grad_feats = call(functools.partial(finish, cap, edge), [flat], (coming, *got), "v" * (count + 1), name="finish")[0]
    return (activated, grad_feats, grad_weight)


def solution(mesh):
    in_specs = (
        P(("rep", "dom"), None),
        P(("rep", "dom"), None),
        P(),
        P(),
        P(("rep", "dom"), None, None, None, None),
        P(("rep", "dom"), None, None),
        P(("rep", "dom"), None, None, None),
        P(("rep", "dom"), None),
        P("rep", "dom", None, None),
    )
    out_specs = (P(("rep", "dom"), None), P(("rep", "dom"), None), P())
    return jax.shard_map(local, mesh=mesh, in_specs=in_specs, out_specs=out_specs, check_vma=False)
```

```python
import functools
import math

import jax
import jax.numpy as jnp
from jax import lax
from jax.experimental import pallas as pl
from jax.experimental.pallas import tpu as pltpu
from jax.sharding import PartitionSpec as P

F32, BF16 = jnp.float32, jnp.bfloat16
ROOT = math.sqrt(2.0 / math.pi)
CUBIC = 0.044715


def swapped(value, axis, k):
    return lax.ppermute(value, axis, [(i, i ^ k) for i in range(lax.axis_size(axis))])


def after(value, other):
    return value if other is None else lax.optimization_barrier((value, other))[0]


def fenced(sure, body, *args):
    blank = lambda *args: jax.tree.map(lambda s: jnp.zeros(s.shape, s.dtype), jax.eval_shape(body, *args))
    return lax.cond(sure, body, blank, *args)


def call(body, outs, args, kinds, scratch=(), flops=0, name=None):
    spaces = {"s": pltpu.SMEM, "v": pltpu.VMEM, "h": pltpu.HBM}
    nbytes = sum(math.prod(a.shape) * a.dtype.itemsize for a in (*args, *outs))
    work = sum(math.prod(s.shape) * jnp.dtype(s.dtype).itemsize for s in scratch if s.memory_space == pltpu.VMEM)
    return pl.pallas_call(
        body,
        out_shape=outs,
        in_specs=[pl.BlockSpec(memory_space=spaces[k]) for k in kinds],
        out_specs=[pl.BlockSpec(memory_space=pltpu.VMEM) for _ in outs],
        scratch_shapes=list(scratch),
        cost_estimate=pl.CostEstimate(flops=flops, bytes_accessed=nbytes, transcendentals=0),
        compiler_params=pltpu.CompilerParams(vmem_limit_bytes=nbytes + work + (4 << 20)),
        name=name,
    )(*args)


def arrange(count, me_ref, cols_ref, in_hbm, a_ref, in_ref, in_sem):
    blocks, _, pairs, edge, _ = in_ref.shape
    rows = blocks * edge
    copies = [pltpu.make_async_copy(in_hbm.at[b], in_ref.at[b], in_sem.at[b]) for b in range(blocks)]
    for copy in copies:
        copy.start()
    a_ref[...] = jnp.zeros_like(a_ref)
    for b in range(blocks):
        copies[b].wait()
        for n in range(count):
            s = me_ref[0] ^ ((count - n) % count)
            for k in range(pairs):
                start = pl.multiple_of(n * rows + cols_ref[b, k, s] * edge, edge)
                a_ref[b * edge:(b + 1) * edge, pl.ds(start, edge)] = in_ref[b, s, k]


def dot(left, right):
    return jnp.dot(left, right, preferred_element_type=F32)


def dot_t(left, right):
    return lax.dot_general(left, right, (((0,), (0,)), ((), ())), preferred_element_type=F32)


def layer(count, doms, me_ref, want_ref, refs_ref, *args):
    panels, others = args[:count], args[count:count + doms - 1]
    (a_ref, off_ref, weight_ref, bias_ref, cot_ref,
     act_ref, keep_ref, give_ref, *rest) = args[count + doms - 1:]
    outs, (grad_ref, term_ref, block_ref) = rest[:count], rest[count:]
    blocks, tiles, edge, _ = off_ref.shape
    rows, cap = blocks * edge, want_ref.shape[0]
    for n in range(1, doms):
        f = me_ref[1] ^ n
        for c in range(cap):
            block_ref[f * cap + c] = others[n - 1][pl.ds(pl.multiple_of(want_ref[c, f] * edge, edge), edge), :]
    inner = dot(a_ref[...], jnp.concatenate([ref[...] for ref in panels], axis=0))
    sums = []
    for b in range(blocks):
        left = jnp.concatenate([off_ref[b, k] for k in range(tiles)], axis=1)
        right = jnp.concatenate([block_ref[refs_ref[b, k]] for k in range(tiles)], axis=0)
        sums.append(inner[b * edge:(b + 1) * edge] + dot(left, right))
    agg = jnp.concatenate(sums, axis=0).astype(BF16)
    v = dot(agg, weight_ref[...]) + bias_ref[...]
    t = jnp.tanh(ROOT * (v + CUBIC * (v * v * v)))
    act_ref[...] = (0.5 * v * (1.0 + t)).astype(BF16)
    slope = 0.5 * (1.0 + t) + 0.5 * v * (1.0 - t * t) * (ROOT * (1.0 + 3.0 * CUBIC * (v * v)))
    grad_pre = (cot_ref[...].astype(F32) * slope).astype(BF16)
    grad_agg = lax.dot_general(
        grad_pre, weight_ref[...], (((1,), (1,)), ((), ())), preferred_element_type=F32).astype(BF16)
    grad_ref[...] = grad_agg
    for n in range(count):
        outs[n][...] = dot_t(a_ref[:, n * rows:(n + 1) * rows], grad_agg).astype(BF16)
    term_ref[...] = dot_t(agg, grad_pre)
    half, core = keep_ref.shape[0], me_ref[1] & 1
    keep_ref[...] = term_ref[pl.ds(pl.multiple_of(core * half, half), half), :].astype(BF16)
    give_ref[...] = term_ref[pl.ds(pl.multiple_of((1 - core) * half, half), half), :].astype(BF16)


def spread_outer(want_ref, refs_ref, off_ref, grad_ref, out_ref, total_ref):
    blocks, tiles, edge, _ = off_ref.shape
    cap, doms = want_ref.shape
    grad_agg = grad_ref[...]
    total_ref[...] = jnp.zeros_like(total_ref)
    for b in range(blocks):
        grad_b = grad_agg[b * edge:(b + 1) * edge]
        for k in range(tiles):
            total_ref[refs_ref[b, k]] += dot_t(off_ref[b, k], grad_b)
    for f in range(doms):
        for c in range(cap):
            out_ref[f, c * edge:(c + 1) * edge, :] = total_ref[f * cap + c].astype(BF16)
            top = cap * edge + c * 16
            out_ref[f, top:top + 16, :] = jnp.full((16, out_ref.shape[2]), want_ref[c, f], jnp.int32).astype(BF16)


def joined(part, axis, k):
    return (part.astype(F32) + swapped(part, axis, k).astype(F32)).astype(BF16)


def finish(cap, edge, scale, me_ref, part_ref, other_ref, coming_ref, *args):
    terms, (out_ref, weight_ref) = args[:-2], args[-2:]
    half, core = part_ref.shape[0], me_ref[1] & 1
    weight_ref[pl.ds(pl.multiple_of(core * half, half), half), :] = (part_ref[...].astype(F32) * scale).astype(BF16)
    weight_ref[pl.ds(pl.multiple_of((1 - core) * half, half), half), :] = (other_ref[...].astype(F32) * scale).astype(BF16)
    for j in range(out_ref.shape[0] // edge):
        part = slice(j * edge, (j + 1) * edge)
        total = terms[0][part, :].astype(F32)
        for ref in terms[1:]:
            total += ref[part, :].astype(F32)
        for f in range(coming_ref.shape[0]):
            for c in range(cap):
                top = cap * edge + c * 16
                place = coming_ref[f, top:top + 1, :].astype(F32)
                total += jnp.where(place == j, coming_ref[f, c * edge:(c + 1) * edge, :].astype(F32), 0.0)
        out_ref[part, :] = total.astype(BF16)


def local(feats, cotangent, weight, bias, in_vals, in_cols, off_vals, off_ref, want):
    count, doms = lax.axis_size("rep"), lax.axis_size("dom")
    me = jnp.stack([lax.axis_index("rep"), lax.axis_index("dom")]).astype(jnp.int32)
    blocks, _, _, edge, _ = in_vals.shape
    rows, width = feats.shape
    requests = want.transpose(0, 1, 3, 2).reshape(want.shape[3], want.shape[2])
    cap = requests.shape[0]
    shape = jax.ShapeDtypeStruct
    flat = shape((rows, width), BF16)

    slots = doms * cap
    sure = requests[0, 0] >= 0
    scale = 1.0 / math.sqrt(rows * count * doms)

    def exchange(outer, part):
        coming = lax.all_to_all(outer, "dom", split_axis=0, concat_axis=0, tiled=True)
        for axis, k, size in (("dom", 4, doms), ("rep", 1, count)):
            while k < size:
                part, k = joined(part, axis, k), 2 * k
        return coming, part, swapped(part, "dom", 1)

    near = swapped(feats, "dom", 1)
    even = [feats] + [swapped(feats, "dom", k) for k in range(2, doms, 2)]
    panels = [feats] + [swapped(feats, "rep", k) for k in range(count - 1, 0, -1)]
    a = call(
        functools.partial(arrange, count), [shape((rows, count * rows), BF16)],
        (after(after(me, near), even[2]), in_cols.transpose(0, 2, 1), in_vals), "ssh",
        scratch=[pltpu.VMEM(in_vals.shape, BF16), pltpu.SemaphoreType.DMA((blocks,))], name="arrange")[0]
    odd = [near] + [swapped(after(after(value, a), panels[1]), "dom", 1) for n, value in enumerate(even) if n]
    others = [value for pair in zip(even, odd) for value in pair][1:]
    activated, keep, give, *terms, grad_agg = call(
        functools.partial(layer, count, doms),
        [flat] + [shape((width // 2, width), BF16)] * 2 + [flat] * (count + 1),
        (me, requests, off_ref, *panels, *others, a, off_vals, weight, bias.reshape(1, width), cotangent),
        "sss" + "v" * (count + doms + 4),
        scratch=[pltpu.VMEM((width, width), F32), pltpu.VMEM((slots, edge, width), BF16)],
        flops=10**9, name="layer")
    part = (keep.astype(F32) + swapped(give, "dom", 1).astype(F32)).astype(BF16)
    part = joined(part, "dom", 2)
    got = [terms[0]] + [swapped(terms[count - k], "rep", k) for k in range(count - 1, 0, -1)]
    outer = call(
        spread_outer, [shape((doms, cap * (edge + 16), width), BF16)], (requests, off_ref, off_vals, grad_agg), "ssvv",
        scratch=[pltpu.VMEM((slots, edge, width), F32)], flops=10**9, name="outer")[0]
    coming, part, other = fenced(sure, exchange, outer, part)
    grad_feats, grad_weight = call(
        functools.partial(finish, cap, edge, scale), [flat, shape((width, width), BF16)],
        (me, part, other, coming, *got), "s" + "v" * (count + 3), name="finish")
    return (activated, grad_feats, grad_weight)


def solution(mesh):
    in_specs = (
        P(("rep", "dom"), None),
        P(("rep", "dom"), None),
        P(),
        P(),
        P(("rep", "dom"), None, None, None, None),
        P(("rep", "dom"), None, None),
        P(("rep", "dom"), None, None, None),
        P(("rep", "dom"), None),
        P("rep", "dom", None, None),
    )
    out_specs = (P(("rep", "dom"), None), P(("rep", "dom"), None), P())
    return jax.shard_map(local, mesh=mesh, in_specs=in_specs, out_specs=out_specs, check_vma=False)
```

```python
import functools
import math

import jax
import jax.numpy as jnp
from jax import lax
from jax.experimental import pallas as pl
from jax.experimental.pallas import tpu as pltpu
from jax.sharding import PartitionSpec as P

F32, BF16 = jnp.float32, jnp.bfloat16
ROOT = math.sqrt(2.0 / math.pi)
CUBIC = 0.044715


def swapped(value, axis, k):
    return lax.ppermute(value, axis, [(i, i ^ k) for i in range(lax.axis_size(axis))])


def relayed(value, turns):
    pairs = [(0, 1), (1, 3), (3, 2), (2, 0)]
    return lax.ppermute(value, "rep", [pair[::turns] for pair in pairs])


def after(value, other):
    return value if other is None else lax.optimization_barrier((value, other))[0]


def fenced(sure, body, *args):
    blank = lambda *args: jax.tree.map(lambda s: jnp.zeros(s.shape, s.dtype), jax.eval_shape(body, *args))
    return lax.cond(sure, body, blank, *args)


def call(body, outs, args, kinds, scratch=(), flops=0, name=None):
    spaces = {"s": pltpu.SMEM, "v": pltpu.VMEM, "h": pltpu.HBM}
    nbytes = sum(math.prod(a.shape) * a.dtype.itemsize for a in (*args, *outs))
    work = sum(math.prod(s.shape) * jnp.dtype(s.dtype).itemsize for s in scratch if s.memory_space == pltpu.VMEM)
    return pl.pallas_call(
        body,
        out_shape=outs,
        in_specs=[pl.BlockSpec(memory_space=spaces[k]) for k in kinds],
        out_specs=[pl.BlockSpec(memory_space=pltpu.VMEM) for _ in outs],
        scratch_shapes=list(scratch),
        cost_estimate=pl.CostEstimate(flops=flops, bytes_accessed=nbytes, transcendentals=0),
        compiler_params=pltpu.CompilerParams(vmem_limit_bytes=nbytes + work + (4 << 20)),
        name=name,
    )(*args)


def arrange(count, me_ref, cols_ref, in_hbm, a_ref, in_ref, in_sem):
    blocks, _, pairs, edge, _ = in_ref.shape
    rows = blocks * edge
    copies = [pltpu.make_async_copy(in_hbm.at[b], in_ref.at[b], in_sem.at[b]) for b in range(blocks)]
    for copy in copies:
        copy.start()
    a_ref[...] = jnp.zeros_like(a_ref)
    for b in range(blocks):
        copies[b].wait()
        for n in range(count):
            s = me_ref[0] ^ ((count - n) % count)
            for k in range(pairs):
                start = pl.multiple_of(n * rows + cols_ref[b, k, s] * edge, edge)
                a_ref[b * edge:(b + 1) * edge, pl.ds(start, edge)] = in_ref[b, s, k]


def dot(left, right):
    return jnp.dot(left, right, preferred_element_type=F32)


def dot_t(left, right):
    return lax.dot_general(left, right, (((0,), (0,)), ((), ())), preferred_element_type=F32)


def layer(count, doms, me_ref, want_ref, refs_ref, *args):
    panels, others = args[:count], args[count:count + doms - 1]
    (a_ref, off_ref, weight_ref, bias_ref, cot_ref,
     act_ref, keep_ref, give_ref, *rest) = args[count + doms - 1:]
    outs, (grad_ref, term_ref, block_ref) = rest[:count], rest[count:]
    blocks, tiles, edge, _ = off_ref.shape
    rows, cap = blocks * edge, want_ref.shape[0]
    for n in range(1, doms):
        f = me_ref[1] ^ n
        for c in range(cap):
            block_ref[f * cap + c] = others[n - 1][pl.ds(pl.multiple_of(want_ref[c, f] * edge, edge), edge), :]
    inner = dot(a_ref[...], jnp.concatenate([ref[...] for ref in panels], axis=0))
    sums = []
    for b in range(blocks):
        left = jnp.concatenate([off_ref[b, k] for k in range(tiles)], axis=1)
        right = jnp.concatenate([block_ref[refs_ref[b, k]] for k in range(tiles)], axis=0)
        sums.append(inner[b * edge:(b + 1) * edge] + dot(left, right))
    agg = jnp.concatenate(sums, axis=0).astype(BF16)
    v = dot(agg, weight_ref[...]) + bias_ref[...]
    t = jnp.tanh(ROOT * (v + CUBIC * (v * v * v)))
    act_ref[...] = (0.5 * v * (1.0 + t)).astype(BF16)
    slope = 0.5 * (1.0 + t) + 0.5 * v * (1.0 - t * t) * (ROOT * (1.0 + 3.0 * CUBIC * (v * v)))
    grad_pre = (cot_ref[...].astype(F32) * slope).astype(BF16)
    grad_agg = lax.dot_general(
        grad_pre, weight_ref[...], (((1,), (1,)), ((), ())), preferred_element_type=F32).astype(BF16)
    grad_ref[...] = grad_agg
    for n in range(count):
        outs[n][...] = dot_t(a_ref[:, n * rows:(n + 1) * rows], grad_agg).astype(BF16)
    term_ref[...] = dot_t(agg, grad_pre)
    half, core = keep_ref.shape[0], me_ref[1] & 1
    keep_ref[...] = term_ref[pl.ds(pl.multiple_of(core * half, half), half), :].astype(BF16)
    give_ref[...] = term_ref[pl.ds(pl.multiple_of((1 - core) * half, half), half), :].astype(BF16)


def spread_outer(want_ref, refs_ref, off_ref, grad_ref, out_ref, total_ref):
    blocks, tiles, edge, _ = off_ref.shape
    cap, doms = want_ref.shape
    grad_agg = grad_ref[...]
    total_ref[...] = jnp.zeros_like(total_ref)
    for b in range(blocks):
        grad_b = grad_agg[b * edge:(b + 1) * edge]
        for k in range(tiles):
            total_ref[refs_ref[b, k]] += dot_t(off_ref[b, k], grad_b)
    for f in range(doms):
        for c in range(cap):
            out_ref[f, c * edge:(c + 1) * edge, :] = total_ref[f * cap + c].astype(BF16)
            top = cap * edge + c * 16
            out_ref[f, top:top + 16, :] = jnp.full((16, out_ref.shape[2]), want_ref[c, f], jnp.int32).astype(BF16)


def joined(part, axis, k):
    return (part.astype(F32) + swapped(part, axis, k).astype(F32)).astype(BF16)


def finish(cap, edge, scale, me_ref, part_ref, other_ref, coming_ref, *args):
    terms, (out_ref, weight_ref) = args[:-2], args[-2:]
    half, core = part_ref.shape[0], me_ref[1] & 1
    weight_ref[pl.ds(pl.multiple_of(core * half, half), half), :] = (part_ref[...].astype(F32) * scale).astype(BF16)
    weight_ref[pl.ds(pl.multiple_of((1 - core) * half, half), half), :] = (other_ref[...].astype(F32) * scale).astype(BF16)
    for j in range(out_ref.shape[0] // edge):
        part = slice(j * edge, (j + 1) * edge)
        total = terms[0][part, :].astype(F32)
        for ref in terms[1:]:
            total += ref[part, :].astype(F32)
        for f in range(coming_ref.shape[0]):
            for c in range(cap):
                top = cap * edge + c * 16
                place = coming_ref[f, top:top + 1, :].astype(F32)
                total += jnp.where(place == j, coming_ref[f, c * edge:(c + 1) * edge, :].astype(F32), 0.0)
        out_ref[part, :] = total.astype(BF16)


def local(feats, cotangent, weight, bias, in_vals, in_cols, off_vals, off_ref, want):
    count, doms = lax.axis_size("rep"), lax.axis_size("dom")
    me = jnp.stack([lax.axis_index("rep"), lax.axis_index("dom")]).astype(jnp.int32)
    blocks, _, _, edge, _ = in_vals.shape
    rows, width = feats.shape
    requests = want.transpose(0, 1, 3, 2).reshape(want.shape[3], want.shape[2])
    cap = requests.shape[0]
    shape = jax.ShapeDtypeStruct
    flat = shape((rows, width), BF16)

    slots = doms * cap
    sure = requests[0, 0] >= 0
    scale = 1.0 / math.sqrt(rows * count * doms)

    def exchange(outer, part):
        coming = lax.all_to_all(outer, "dom", split_axis=0, concat_axis=0, tiled=True)
        for axis, k, size in (("dom", 4, doms), ("rep", 1, count)):
            while k < size:
                part, k = joined(part, axis, k), 2 * k
        return coming, part, swapped(part, "dom", 1)

    near = swapped(feats, "dom", 1)
    even = [feats] + [swapped(feats if k == 4 else after(feats, near), "dom", k) for k in range(2, doms, 2)]
    inside = (lax.axis_index("rep") == 1) | (lax.axis_index("rep") == 2)
    if count == 4:
        far = swapped(feats, "rep", 3)
        panels = [feats, far, relayed(jnp.where(inside, far, feats), -1), swapped(feats, "rep", 1)]
    else:
        panels = [feats] + [swapped(feats, "rep", k) for k in range(count - 1, 0, -1)]
    a = call(
        functools.partial(arrange, count), [shape((rows, count * rows), BF16)],
        (after(after(me, near), even[2]), in_cols.transpose(0, 2, 1), in_vals), "ssh",
        scratch=[pltpu.VMEM(in_vals.shape, BF16), pltpu.SemaphoreType.DMA((blocks,))], name="arrange")[0]
    odd = [near] + [swapped(after(value, a), "dom", 1) for n, value in enumerate(even) if n]
    others = [value for pair in zip(even, odd) for value in pair][1:]
    activated, keep, give, *terms, grad_agg = call(
        functools.partial(layer, count, doms),
        [flat] + [shape((width // 2, width), BF16)] * 2 + [flat] * (count + 1),
        (me, requests, off_ref, *panels, *others, a, off_vals, weight, bias.reshape(1, width), cotangent),
        "sss" + "v" * (count + doms + 4),
        scratch=[pltpu.VMEM((width, width), F32), pltpu.VMEM((slots, edge, width), BF16)],
        flops=10**9, name="layer")
    part = (keep.astype(F32) + swapped(give, "dom", 1).astype(F32)).astype(BF16)
    first = part
    part = joined(part, "dom", 2)
    got = [terms[0]] + [swapped(after(terms[count - k], first if k == 1 else None), "rep", k) for k in range(count - 1, 0, -1)]
    outer = call(
        spread_outer, [shape((doms, cap * (edge + 16), width), BF16)], (requests, off_ref, off_vals, grad_agg), "ssvv",
        scratch=[pltpu.VMEM((slots, edge, width), F32)], flops=10**9, name="outer")[0]
    coming, part, other = fenced(sure, exchange, outer, part)
    grad_feats, grad_weight = call(
        functools.partial(finish, cap, edge, scale), [flat, shape((width, width), BF16)],
        (me, part, other, coming, *got), "s" + "v" * (count + 3), name="finish")
    return (activated, grad_feats, grad_weight)


def solution(mesh):
    in_specs = (
        P(("rep", "dom"), None),
        P(("rep", "dom"), None),
        P(),
        P(),
        P(("rep", "dom"), None, None, None, None),
        P(("rep", "dom"), None, None),
        P(("rep", "dom"), None, None, None),
        P(("rep", "dom"), None),
        P("rep", "dom", None, None),
    )
    out_specs = (P(("rep", "dom"), None), P(("rep", "dom"), None), P())
    return jax.shard_map(local, mesh=mesh, in_specs=in_specs, out_specs=out_specs, check_vma=False)
```

```python
import functools
import math

import jax
import jax.numpy as jnp
from jax import lax
from jax.experimental import pallas as pl
from jax.experimental.pallas import tpu as pltpu
from jax.sharding import PartitionSpec as P

F32, BF16 = jnp.float32, jnp.bfloat16
ROOT = math.sqrt(2.0 / math.pi)
CUBIC = 0.044715


def swapped(value, axis, k):
    return lax.ppermute(value, axis, [(i, i ^ k) for i in range(lax.axis_size(axis))])


def relayed(value, turns):
    pairs = [(0, 1), (1, 3), (3, 2), (2, 0)]
    return lax.ppermute(value, "rep", [pair[::turns] for pair in pairs])


def after(value, other):
    return value if other is None else lax.optimization_barrier((value, other))[0]


def fenced(sure, body, *args):
    blank = lambda *args: jax.tree.map(lambda s: jnp.zeros(s.shape, s.dtype), jax.eval_shape(body, *args))
    return lax.cond(sure, body, blank, *args)


def call(body, outs, args, kinds, scratch=(), flops=0, name=None):
    spaces = {"s": pltpu.SMEM, "v": pltpu.VMEM, "h": pltpu.HBM}
    nbytes = sum(math.prod(a.shape) * a.dtype.itemsize for a in (*args, *outs))
    work = sum(math.prod(s.shape) * jnp.dtype(s.dtype).itemsize for s in scratch if s.memory_space == pltpu.VMEM)
    return pl.pallas_call(
        body,
        out_shape=outs,
        in_specs=[pl.BlockSpec(memory_space=spaces[k]) for k in kinds],
        out_specs=[pl.BlockSpec(memory_space=pltpu.VMEM) for _ in outs],
        scratch_shapes=list(scratch),
        cost_estimate=pl.CostEstimate(flops=flops, bytes_accessed=nbytes, transcendentals=0),
        compiler_params=pltpu.CompilerParams(vmem_limit_bytes=nbytes + work + (4 << 20)),
        name=name,
    )(*args)


def arrange(count, me_ref, cols_ref, in_hbm, a_ref, in_ref, in_sem):
    blocks, _, pairs, edge, _ = in_ref.shape
    rows = blocks * edge
    copies = [pltpu.make_async_copy(in_hbm.at[b], in_ref.at[b], in_sem.at[b]) for b in range(blocks)]
    for copy in copies:
        copy.start()
    a_ref[...] = jnp.zeros_like(a_ref)
    for b in range(blocks):
        copies[b].wait()
        for n in range(count):
            s = me_ref[0] ^ ((count - n) % count)
            for k in range(pairs):
                start = pl.multiple_of(n * rows + cols_ref[b, k, s] * edge, edge)
                a_ref[b * edge:(b + 1) * edge, pl.ds(start, edge)] = in_ref[b, s, k]


def dot(left, right):
    return jnp.dot(left, right, preferred_element_type=F32)


def dot_t(left, right):
    return lax.dot_general(left, right, (((0,), (0,)), ((), ())), preferred_element_type=F32)


def layer(count, doms, me_ref, want_ref, refs_ref, *args):
    panels, others = args[:count], args[count:count + doms - 1]
    (a_ref, off_ref, weight_ref, bias_ref, cot_ref,
     act_ref, keep_ref, give_ref, *rest) = args[count + doms - 1:]
    outs, (grad_ref, term_ref, block_ref) = rest[:count], rest[count:]
    blocks, tiles, edge, _ = off_ref.shape
    rows, cap = blocks * edge, want_ref.shape[0]
    for n in range(1, doms):
        f = me_ref[1] ^ n
        for c in range(cap):
            block_ref[f * cap + c] = others[n - 1][pl.ds(pl.multiple_of(want_ref[c, f] * edge, edge), edge), :]
    inner = dot(a_ref[...], jnp.concatenate([ref[...] for ref in panels], axis=0))
    sums = []
    for b in range(blocks):
        left = jnp.concatenate([off_ref[b, k] for k in range(tiles)], axis=1)
        right = jnp.concatenate([block_ref[refs_ref[b, k]] for k in range(tiles)], axis=0)
        sums.append(inner[b * edge:(b + 1) * edge] + dot(left, right))
    agg = jnp.concatenate(sums, axis=0).astype(BF16)
    v = dot(agg, weight_ref[...]) + bias_ref[...]
    t = jnp.tanh(ROOT * (v + CUBIC * (v * v * v)))
    act_ref[...] = (0.5 * v * (1.0 + t)).astype(BF16)
    slope = 0.5 * (1.0 + t) + 0.5 * v * (1.0 - t * t) * (ROOT * (1.0 + 3.0 * CUBIC * (v * v)))
    grad_pre = (cot_ref[...].astype(F32) * slope).astype(BF16)
    grad_agg = lax.dot_general(
        grad_pre, weight_ref[...], (((1,), (1,)), ((), ())), preferred_element_type=F32).astype(BF16)
    grad_ref[...] = grad_agg
    for n in range(count):
        outs[n][...] = dot_t(a_ref[:, n * rows:(n + 1) * rows], grad_agg).astype(BF16)
    term_ref[...] = dot_t(agg, grad_pre)
    half, core = keep_ref.shape[0], me_ref[1] & 1
    keep_ref[...] = term_ref[pl.ds(pl.multiple_of(core * half, half), half), :].astype(BF16)
    give_ref[...] = term_ref[pl.ds(pl.multiple_of((1 - core) * half, half), half), :].astype(BF16)


def spread_outer(want_ref, refs_ref, off_ref, grad_ref, out_ref, total_ref):
    blocks, tiles, edge, _ = off_ref.shape
    cap, doms = want_ref.shape
    grad_agg = grad_ref[...]
    total_ref[...] = jnp.zeros_like(total_ref)
    for b in range(blocks):
        grad_b = grad_agg[b * edge:(b + 1) * edge]
        for k in range(tiles):
            total_ref[refs_ref[b, k]] += dot_t(off_ref[b, k], grad_b)
    for f in range(doms):
        for c in range(cap):
            out_ref[f, c * edge:(c + 1) * edge, :] = total_ref[f * cap + c].astype(BF16)
            top = cap * edge + c * 16
            out_ref[f, top:top + 16, :] = jnp.full((16, out_ref.shape[2]), want_ref[c, f], jnp.int32).astype(BF16)


def joined(part, axis, k):
    return (part.astype(F32) + swapped(part, axis, k).astype(F32)).astype(BF16)


def join(scale, me_ref, part_ref, other_ref, out_ref):
    half, core = part_ref.shape[0], me_ref[1] & 1
    out_ref[pl.ds(pl.multiple_of(core * half, half), half), :] = (part_ref[...].astype(F32) * scale).astype(BF16)
    out_ref[pl.ds(pl.multiple_of((1 - core) * half, half), half), :] = (other_ref[...].astype(F32) * scale).astype(BF16)


def finish(cap, edge, coming_ref, *args):
    terms, out_ref = args[:-1], args[-1]
    for j in range(out_ref.shape[0] // edge):
        part = slice(j * edge, (j + 1) * edge)
        total = terms[0][part, :].astype(F32)
        for ref in terms[1:]:
            total += ref[part, :].astype(F32)
        for f in range(coming_ref.shape[0]):
            for c in range(cap):
                top = cap * edge + c * 16
                place = coming_ref[f, top:top + 1, :].astype(F32)
                total += jnp.where(place == j, coming_ref[f, c * edge:(c + 1) * edge, :].astype(F32), 0.0)
        out_ref[part, :] = total.astype(BF16)


def local(feats, cotangent, weight, bias, in_vals, in_cols, off_vals, off_ref, want):
    count, doms = lax.axis_size("rep"), lax.axis_size("dom")
    me = jnp.stack([lax.axis_index("rep"), lax.axis_index("dom")]).astype(jnp.int32)
    blocks, _, _, edge, _ = in_vals.shape
    rows, width = feats.shape
    requests = want.transpose(0, 1, 3, 2).reshape(want.shape[3], want.shape[2])
    cap = requests.shape[0]
    shape = jax.ShapeDtypeStruct
    flat = shape((rows, width), BF16)

    slots = doms * cap
    sure = requests[0, 0] >= 0
    scale = 1.0 / math.sqrt(rows * count * doms)

    def exchange(outer, part):
        coming = lax.all_to_all(outer, "dom", split_axis=0, concat_axis=0, tiled=True)
        for axis, k, size in (("dom", 2, 4), ("rep", 1, count)):
            while k < size:
                part, k = joined(part, axis, k), 2 * k
        return coming, call(functools.partial(join, scale), [shape((width, width), BF16)], (me, part, swapped(part, "dom", 1)), "svv", name="join")[0]

    near = swapped(feats, "dom", 1)
    even = [feats] + [swapped(feats if k == 4 else after(feats, near), "dom", k) for k in range(2, doms, 2)]
    inside = (lax.axis_index("rep") == 1) | (lax.axis_index("rep") == 2)
    if count == 4:
        far = swapped(feats, "rep", 3)
        panels = [feats, far, relayed(jnp.where(inside, far, feats), -1), swapped(feats, "rep", 1)]
    else:
        panels = [feats] + [swapped(feats, "rep", k) for k in range(count - 1, 0, -1)]
    a = call(
        functools.partial(arrange, count), [shape((rows, count * rows), BF16)],
        (after(after(me, near), even[2]), in_cols.transpose(0, 2, 1), in_vals), "ssh",
        scratch=[pltpu.VMEM(in_vals.shape, BF16), pltpu.SemaphoreType.DMA((blocks,))], name="arrange")[0]
    odd = [near] + [swapped(after(value, a), "dom", 1) for n, value in enumerate(even) if n]
    others = [value for pair in zip(even, odd) for value in pair][1:]
    activated, keep, give, *terms, grad_agg = call(
        functools.partial(layer, count, doms),
        [flat] + [shape((width // 2, width), BF16)] * 2 + [flat] * (count + 1),
        (me, requests, off_ref, *panels, *others, a, off_vals, weight, bias.reshape(1, width), cotangent),
        "sss" + "v" * (count + doms + 4),
        scratch=[pltpu.VMEM((width, width), F32), pltpu.VMEM((slots, edge, width), BF16)],
        flops=10**9, name="layer")
    part = (keep.astype(F32) + swapped(give, "dom", 1).astype(F32)).astype(BF16)
    first = part
    part = joined(part, "dom", 4)
    got = [terms[0]] + [swapped(after(terms[count - k], first if k == 1 else None), "rep", k) for k in range(count - 1, 0, -1)]
    outer = call(
        spread_outer, [shape((doms, cap * (edge + 16), width), BF16)], (requests, off_ref, off_vals, grad_agg), "ssvv",
        scratch=[pltpu.VMEM((slots, edge, width), F32)], flops=10**9, name="outer")[0]
    coming, grad_weight = fenced(sure, exchange, outer, part)
    grad_feats = call(functools.partial(finish, cap, edge), [flat], (coming, *got), "v" * (count + 1), name="finish")[0]
    return (activated, grad_feats, grad_weight)


def solution(mesh):
    in_specs = (
        P(("rep", "dom"), None),
        P(("rep", "dom"), None),
        P(),
        P(),
        P(("rep", "dom"), None, None, None, None),
        P(("rep", "dom"), None, None),
        P(("rep", "dom"), None, None, None),
        P(("rep", "dom"), None),
        P("rep", "dom", None, None),
    )
    out_specs = (P(("rep", "dom"), None), P(("rep", "dom"), None), P())
    return jax.shard_map(local, mesh=mesh, in_specs=in_specs, out_specs=out_specs, check_vma=False)
```

```python
import functools
import math

import jax
import jax.numpy as jnp
from jax import lax
from jax.experimental import pallas as pl
from jax.experimental.pallas import tpu as pltpu
from jax.sharding import PartitionSpec as P

F32, BF16 = jnp.float32, jnp.bfloat16
ROOT = math.sqrt(2.0 / math.pi)
CUBIC = 0.044715


def turns(count):
    return [0, 3, 1, 2] if count == 4 else [0] + list(range(count - 1, 0, -1))


def swapped(value, axis, k):
    return lax.ppermute(value, axis, [(i, i ^ k) for i in range(lax.axis_size(axis))])


def relayed(value, turns):
    pairs = [(0, 1), (1, 3), (3, 2), (2, 0)]
    return lax.ppermute(value, "rep", [pair[::turns] for pair in pairs])


def after(value, other):
    return value if other is None else lax.optimization_barrier((value, other))[0]


def fenced(sure, body, *args):
    blank = lambda *args: jax.tree.map(lambda s: jnp.zeros(s.shape, s.dtype), jax.eval_shape(body, *args))
    return lax.cond(sure, body, blank, *args)


def call(body, outs, args, kinds, scratch=(), flops=0, name=None):
    spaces = {"s": pltpu.SMEM, "v": pltpu.VMEM, "h": pltpu.HBM}
    nbytes = sum(math.prod(a.shape) * a.dtype.itemsize for a in (*args, *outs))
    work = sum(math.prod(s.shape) * jnp.dtype(s.dtype).itemsize for s in scratch if s.memory_space == pltpu.VMEM)
    return pl.pallas_call(
        body,
        out_shape=outs,
        in_specs=[pl.BlockSpec(memory_space=spaces[k]) for k in kinds],
        out_specs=[pl.BlockSpec(memory_space=pltpu.VMEM) for _ in outs],
        scratch_shapes=list(scratch),
        cost_estimate=pl.CostEstimate(flops=flops, bytes_accessed=nbytes, transcendentals=0),
        compiler_params=pltpu.CompilerParams(vmem_limit_bytes=nbytes + work + (4 << 20)),
        name=name,
    )(*args)


def arrange(count, me_ref, cols_ref, in_hbm, a_ref, in_ref, in_sem):
    blocks, _, pairs, edge, _ = in_ref.shape
    rows = blocks * edge
    copies = [pltpu.make_async_copy(in_hbm.at[b], in_ref.at[b], in_sem.at[b]) for b in range(blocks)]
    for copy in copies:
        copy.start()
    a_ref[...] = jnp.zeros_like(a_ref)
    for b in range(blocks):
        copies[b].wait()
        for n in range(count):
            s = me_ref[0] ^ turns(count)[n]
            for k in range(pairs):
                start = pl.multiple_of(n * rows + cols_ref[b, k, s] * edge, edge)
                a_ref[b * edge:(b + 1) * edge, pl.ds(start, edge)] = in_ref[b, s, k]


def dot(left, right):
    return jnp.dot(left, right, preferred_element_type=F32)


def dot_t(left, right):
    return lax.dot_general(left, right, (((0,), (0,)), ((), ())), preferred_element_type=F32)


def begin(a_ref, *args):
    panels, sum_ref = args[:-1], args[-1]
    rows = sum_ref.shape[0]
    sum_ref[...] = dot(a_ref[:, :len(panels) * rows], jnp.concatenate([ref[...] for ref in panels], axis=0))


def layer(count, doms, me_ref, want_ref, refs_ref, *args):
    last_ref, sum_ref, others = args[0], args[1], args[2:doms + 1]
    (a_ref, off_ref, weight_ref, bias_ref, cot_ref,
     act_ref, keep_ref, give_ref, *rest) = args[doms + 1:]
    outs, (grad_ref, term_ref, block_ref) = rest[:count], rest[count:]
    blocks, tiles, edge, _ = off_ref.shape
    rows, cap = blocks * edge, want_ref.shape[0]
    for n in range(1, doms):
        f = me_ref[1] ^ n
        for c in range(cap):
            block_ref[f * cap + c] = others[n - 1][pl.ds(pl.multiple_of(want_ref[c, f] * edge, edge), edge), :]
    inner = sum_ref[...] + dot(a_ref[:, (count - 1) * rows:], last_ref[...])
    sums = []
    for b in range(blocks):
        left = jnp.concatenate([off_ref[b, k] for k in range(tiles)], axis=1)
        right = jnp.concatenate([block_ref[refs_ref[b, k]] for k in range(tiles)], axis=0)
        sums.append(inner[b * edge:(b + 1) * edge] + dot(left, right))
    agg = jnp.concatenate(sums, axis=0).astype(BF16)
    v = dot(agg, weight_ref[...]) + bias_ref[...]
    t = jnp.tanh(ROOT * (v + CUBIC * (v * v * v)))
    act_ref[...] = (0.5 * v * (1.0 + t)).astype(BF16)
    slope = 0.5 * (1.0 + t) + 0.5 * v * (1.0 - t * t) * (ROOT * (1.0 + 3.0 * CUBIC * (v * v)))
    grad_pre = (cot_ref[...].astype(F32) * slope).astype(BF16)
    grad_agg = lax.dot_general(
        grad_pre, weight_ref[...], (((1,), (1,)), ((), ())), preferred_element_type=F32).astype(BF16)
    grad_ref[...] = grad_agg
    for n in range(count):
        outs[n][...] = dot_t(a_ref[:, n * rows:(n + 1) * rows], grad_agg).astype(BF16)
    term_ref[...] = dot_t(agg, grad_pre)
    half, core = keep_ref.shape[0], me_ref[1] & 1
    keep_ref[...] = term_ref[pl.ds(pl.multiple_of(core * half, half), half), :].astype(BF16)
    give_ref[...] = term_ref[pl.ds(pl.multiple_of((1 - core) * half, half), half), :].astype(BF16)


def spread_outer(want_ref, refs_ref, off_ref, grad_ref, out_ref, total_ref):
    blocks, tiles, edge, _ = off_ref.shape
    cap, doms = want_ref.shape
    grad_agg = grad_ref[...]
    total_ref[...] = jnp.zeros_like(total_ref)
    for b in range(blocks):
        grad_b = grad_agg[b * edge:(b + 1) * edge]
        for k in range(tiles):
            total_ref[refs_ref[b, k]] += dot_t(off_ref[b, k], grad_b)
    for f in range(doms):
        for c in range(cap):
            out_ref[f, c * edge:(c + 1) * edge, :] = total_ref[f * cap + c].astype(BF16)
            top = cap * edge + c * 16
            out_ref[f, top:top + 16, :] = jnp.full((16, out_ref.shape[2]), want_ref[c, f], jnp.int32).astype(BF16)


def joined(part, axis, k):
    return (part.astype(F32) + swapped(part, axis, k).astype(F32)).astype(BF16)


def join(scale, me_ref, part_ref, other_ref, out_ref):
    half, core = part_ref.shape[0], me_ref[1] & 1
    out_ref[pl.ds(pl.multiple_of(core * half, half), half), :] = (part_ref[...].astype(F32) * scale).astype(BF16)
    out_ref[pl.ds(pl.multiple_of((1 - core) * half, half), half), :] = (other_ref[...].astype(F32) * scale).astype(BF16)


def finish(cap, edge, coming_ref, *args):
    terms, out_ref = args[:-1], args[-1]
    for j in range(out_ref.shape[0] // edge):
        part = slice(j * edge, (j + 1) * edge)
        total = terms[0][part, :].astype(F32)
        for ref in terms[1:]:
            total += ref[part, :].astype(F32)
        for f in range(coming_ref.shape[0]):
            for c in range(cap):
                top = cap * edge + c * 16
                place = coming_ref[f, top:top + 1, :].astype(F32)
                total += jnp.where(place == j, coming_ref[f, c * edge:(c + 1) * edge, :].astype(F32), 0.0)
        out_ref[part, :] = total.astype(BF16)


def local(feats, cotangent, weight, bias, in_vals, in_cols, off_vals, off_ref, want):
    count, doms = lax.axis_size("rep"), lax.axis_size("dom")
    me = jnp.stack([lax.axis_index("rep"), lax.axis_index("dom")]).astype(jnp.int32)
    blocks, _, _, edge, _ = in_vals.shape
    rows, width = feats.shape
    requests = want.transpose(0, 1, 3, 2).reshape(want.shape[3], want.shape[2])
    cap = requests.shape[0]
    shape = jax.ShapeDtypeStruct
    flat = shape((rows, width), BF16)

    slots = doms * cap
    sure = requests[0, 0] >= 0
    scale = 1.0 / math.sqrt(rows * count * doms)

    def exchange(outer, part, one):
        one = swapped(one, "rep", 1)
        coming = lax.all_to_all(outer, "dom", split_axis=0, concat_axis=0, tiled=True)
        for axis, k, size in (("dom", 2, 4), ("rep", 1, count)):
            while k < size:
                part, k = joined(part, axis, k), 2 * k
        return coming, one, call(functools.partial(join, scale), [shape((width, width), BF16)], (me, part, swapped(part, "dom", 1)), "svv", name="join")[0]

    near = swapped(feats, "dom", 1)
    even = [feats] + [swapped(feats if k == 4 else after(feats, near), "dom", k) for k in range(2, doms, 2)]
    inside = (lax.axis_index("rep") == 1) | (lax.axis_index("rep") == 2)
    if count == 4:
        far = swapped(feats, "rep", 3)
        two = relayed(jnp.where(inside, far, feats), -1)
        panels = [feats, far, swapped(feats, "rep", 1), two]
    else:
        panels = [feats] + [swapped(feats, "rep", k) for k in range(count - 1, 0, -1)]
    a = call(
        functools.partial(arrange, count), [shape((rows, count * rows), BF16)],
        (after(after(me, near), even[2]), in_cols.transpose(0, 2, 1), in_vals), "ssh",
        scratch=[pltpu.VMEM(in_vals.shape, BF16), pltpu.SemaphoreType.DMA((blocks,))], name="arrange")[0]
    odd = [near] + [swapped(after(value, a), "dom", 1) for n, value in enumerate(even) if n]
    others = [value for pair in zip(even, odd) for value in pair][1:]
    begun = call(begin, [shape((rows, width), F32)], (a, *panels[:-1]), "v" * count, name="begin")[0]
    activated, keep, give, *terms, grad_agg = call(
        functools.partial(layer, count, doms),
        [flat] + [shape((width // 2, width), BF16)] * 2 + [flat] * (count + 1),
        (me, requests, off_ref, panels[-1], begun, *others, a, off_vals, weight, bias.reshape(1, width), cotangent),
        "sss" + "v" * (doms + 6),
        scratch=[pltpu.VMEM((width, width), F32), pltpu.VMEM((slots, edge, width), BF16)],
        flops=10**9, name="layer")
    part = (keep.astype(F32) + swapped(give, "dom", 1).astype(F32)).astype(BF16)
    first = part
    part = joined(part, "dom", 4)
    got = [terms[0]] + [swapped(after(terms[turns(count).index(k)], first if k == 2 else None), "rep", k) for k in range(count - 1, 1, -1)]
    outer = call(
        spread_outer, [shape((doms, cap * (edge + 16), width), BF16)], (requests, off_ref, off_vals, grad_agg), "ssvv",
        scratch=[pltpu.VMEM((slots, edge, width), F32)], flops=10**9, name="outer")[0]
    coming, one, grad_weight = fenced(sure, exchange, outer, part, terms[turns(count).index(1)])
    grad_feats = call(functools.partial(finish, cap, edge), [flat], (coming, *got, one), "v" * (count + 1), name="finish")[0]
    return (activated, grad_feats, grad_weight)


def solution(mesh):
    in_specs = (
        P(("rep", "dom"), None),
        P(("rep", "dom"), None),
        P(),
        P(),
        P(("rep", "dom"), None, None, None, None),
        P(("rep", "dom"), None, None),
        P(("rep", "dom"), None, None, None),
        P(("rep", "dom"), None),
        P("rep", "dom", None, None),
    )
    out_specs = (P(("rep", "dom"), None), P(("rep", "dom"), None), P())
    return jax.shard_map(local, mesh=mesh, in_specs=in_specs, out_specs=out_specs, check_vma=False)
```

```python
import functools
import math

import jax
import jax.numpy as jnp
from jax import lax
from jax.experimental import pallas as pl
from jax.experimental.pallas import tpu as pltpu
from jax.sharding import PartitionSpec as P

F32, BF16 = jnp.float32, jnp.bfloat16
ROOT = math.sqrt(2.0 / math.pi)
CUBIC = 0.044715


def turns(count):
    return [0, 3, 1, 2] if count == 4 else [0] + list(range(count - 1, 0, -1))


def swapped(value, axis, k):
    return lax.ppermute(value, axis, [(i, i ^ k) for i in range(lax.axis_size(axis))])


def relayed(value, turns):
    pairs = [(0, 1), (1, 3), (3, 2), (2, 0)]
    return lax.ppermute(value, "rep", [pair[::turns] for pair in pairs])


def after(value, other):
    return value if other is None else lax.optimization_barrier((value, other))[0]


def fenced(sure, body, *args):
    blank = lambda *args: jax.tree.map(lambda s: jnp.zeros(s.shape, s.dtype), jax.eval_shape(body, *args))
    return lax.cond(sure, body, blank, *args)


def call(body, outs, args, kinds, scratch=(), flops=0, name=None):
    spaces = {"s": pltpu.SMEM, "v": pltpu.VMEM, "h": pltpu.HBM}
    nbytes = sum(math.prod(a.shape) * a.dtype.itemsize for a in (*args, *outs))
    work = sum(math.prod(s.shape) * jnp.dtype(s.dtype).itemsize for s in scratch if s.memory_space == pltpu.VMEM)
    return pl.pallas_call(
        body,
        out_shape=outs,
        in_specs=[pl.BlockSpec(memory_space=spaces[k]) for k in kinds],
        out_specs=[pl.BlockSpec(memory_space=pltpu.VMEM) for _ in outs],
        scratch_shapes=list(scratch),
        cost_estimate=pl.CostEstimate(flops=flops, bytes_accessed=nbytes, transcendentals=0),
        compiler_params=pltpu.CompilerParams(vmem_limit_bytes=nbytes + work + (4 << 20)),
        name=name,
    )(*args)


def arrange(count, me_ref, cols_ref, in_hbm, a_ref, in_ref, in_sem):
    blocks, _, pairs, edge, _ = in_ref.shape
    rows = blocks * edge
    copies = [pltpu.make_async_copy(in_hbm.at[b], in_ref.at[b], in_sem.at[b]) for b in range(blocks)]
    for copy in copies:
        copy.start()
    a_ref[...] = jnp.zeros_like(a_ref)
    for b in range(blocks):
        copies[b].wait()
        for n in range(count):
            s = me_ref[0] ^ turns(count)[n]
            for k in range(pairs):
                start = pl.multiple_of(n * rows + cols_ref[b, k, s] * edge, edge)
                a_ref[b * edge:(b + 1) * edge, pl.ds(start, edge)] = in_ref[b, s, k]


def dot(left, right):
    return jnp.dot(left, right, preferred_element_type=F32)


def dot_t(left, right):
    return lax.dot_general(left, right, (((0,), (0,)), ((), ())), preferred_element_type=F32)


def begin(a_ref, *args):
    panels, sum_ref = args[:-1], args[-1]
    rows = sum_ref.shape[0]
    sum_ref[...] = dot(a_ref[:, :len(panels) * rows], jnp.concatenate([ref[...] for ref in panels], axis=0))


def layer(count, doms, me_ref, want_ref, refs_ref, *args):
    last_ref, sum_ref, others = args[0], args[1], args[2:doms + 1]
    (a_ref, off_ref, weight_ref, bias_ref, cot_ref,
     act_ref, keep_ref, give_ref, *rest) = args[doms + 1:]
    outs, (grad_ref, term_ref, block_ref) = rest[:-3], rest[-3:]
    blocks, tiles, edge, _ = off_ref.shape
    rows, cap = blocks * edge, want_ref.shape[0]
    for n in range(1, doms):
        f = me_ref[1] ^ n
        for c in range(cap):
            block_ref[f * cap + c] = others[n - 1][pl.ds(pl.multiple_of(want_ref[c, f] * edge, edge), edge), :]
    inner = sum_ref[...] + dot(a_ref[:, (count - 1) * rows:], last_ref[...])
    sums = []
    for b in range(blocks):
        left = jnp.concatenate([off_ref[b, k] for k in range(tiles)], axis=1)
        right = jnp.concatenate([block_ref[refs_ref[b, k]] for k in range(tiles)], axis=0)
        sums.append(inner[b * edge:(b + 1) * edge] + dot(left, right))
    agg = jnp.concatenate(sums, axis=0).astype(BF16)
    v = dot(agg, weight_ref[...]) + bias_ref[...]
    t = jnp.tanh(ROOT * (v + CUBIC * (v * v * v)))
    act_ref[...] = (0.5 * v * (1.0 + t)).astype(BF16)
    slope = 0.5 * (1.0 + t) + 0.5 * v * (1.0 - t * t) * (ROOT * (1.0 + 3.0 * CUBIC * (v * v)))
    grad_pre = (cot_ref[...].astype(F32) * slope).astype(BF16)
    grad_agg = lax.dot_general(
        grad_pre, weight_ref[...], (((1,), (1,)), ((), ())), preferred_element_type=F32).astype(BF16)
    grad_ref[...] = grad_agg
    for out, n in zip(outs, [n for n, k in enumerate(turns(count)) if k > 2]):
        out[...] = dot_t(a_ref[:, n * rows:(n + 1) * rows], grad_agg).astype(BF16)
    term_ref[...] = dot_t(agg, grad_pre)
    half, core = keep_ref.shape[0], me_ref[1] & 1
    keep_ref[...] = term_ref[pl.ds(pl.multiple_of(core * half, half), half), :].astype(BF16)
    give_ref[...] = term_ref[pl.ds(pl.multiple_of((1 - core) * half, half), half), :].astype(BF16)


def spread_rest(want_ref, refs_ref, a_ref, off_ref, grad_ref, own_ref, near_ref, next_ref, out_ref, total_ref):
    blocks, tiles, edge, _ = off_ref.shape
    cap, doms = want_ref.shape
    grad_agg = grad_ref[...]
    rows = grad_agg.shape[0]
    order = turns(a_ref.shape[1] // rows)
    for ref, n in ((own_ref, order.index(0)), (near_ref, order.index(1)), (next_ref, order.index(2))):
        ref[...] = dot_t(a_ref[:, n * rows:(n + 1) * rows], grad_agg).astype(BF16)
    total_ref[...] = jnp.zeros_like(total_ref)
    for b in range(blocks):
        grad_b = grad_agg[b * edge:(b + 1) * edge]
        for k in range(tiles):
            total_ref[refs_ref[b, k]] += dot_t(off_ref[b, k], grad_b)
    for f in range(doms):
        for c in range(cap):
            out_ref[f, c * edge:(c + 1) * edge, :] = total_ref[f * cap + c].astype(BF16)
            top = cap * edge + c * 16
            out_ref[f, top:top + 16, :] = jnp.full((16, out_ref.shape[2]), want_ref[c, f], jnp.int32).astype(BF16)


def joined(part, axis, k):
    return (part.astype(F32) + swapped(part, axis, k).astype(F32)).astype(BF16)


def join(scale, me_ref, part_ref, other_ref, out_ref):
    half, core = part_ref.shape[0], me_ref[1] & 1
    out_ref[pl.ds(pl.multiple_of(core * half, half), half), :] = (part_ref[...].astype(F32) * scale).astype(BF16)
    out_ref[pl.ds(pl.multiple_of((1 - core) * half, half), half), :] = (other_ref[...].astype(F32) * scale).astype(BF16)


def finish(cap, edge, coming_ref, *args):
    terms, out_ref = args[:-1], args[-1]
    for j in range(out_ref.shape[0] // edge):
        part = slice(j * edge, (j + 1) * edge)
        total = terms[0][part, :].astype(F32)
        for ref in terms[1:]:
            total += ref[part, :].astype(F32)
        for f in range(coming_ref.shape[0]):
            for c in range(cap):
                top = cap * edge + c * 16
                place = coming_ref[f, top:top + 1, :].astype(F32)
                total += jnp.where(place == j, coming_ref[f, c * edge:(c + 1) * edge, :].astype(F32), 0.0)
        out_ref[part, :] = total.astype(BF16)


def local(feats, cotangent, weight, bias, in_vals, in_cols, off_vals, off_ref, want):
    count, doms = lax.axis_size("rep"), lax.axis_size("dom")
    me = jnp.stack([lax.axis_index("rep"), lax.axis_index("dom")]).astype(jnp.int32)
    blocks, _, _, edge, _ = in_vals.shape
    rows, width = feats.shape
    requests = want.transpose(0, 1, 3, 2).reshape(want.shape[3], want.shape[2])
    cap = requests.shape[0]
    shape = jax.ShapeDtypeStruct
    flat = shape((rows, width), BF16)

    slots = doms * cap
    sure = requests[0, 0] >= 0
    scale = 1.0 / math.sqrt(rows * count * doms)

    dom_steps = [k for k in (4, 2) if k < doms] + [1 << n for n in range(3, doms.bit_length() - 1)]

    def exchange(outer, part, one):
        one = swapped(one, "rep", 1)
        coming = lax.all_to_all(outer, "dom", split_axis=0, concat_axis=0, tiled=True)
        for axis, steps in (("dom", dom_steps[1:]), ("rep", [1 << n for n in range(count.bit_length() - 1)])):
            for k in steps:
                part = joined(part, axis, k)
        return coming, one, call(functools.partial(join, scale), [shape((width, width), BF16)], (me, part, swapped(part, "dom", 1)), "svv", name="join")[0]

    near = swapped(feats, "dom", 1)
    even = [feats] + [swapped(feats if k == 4 else after(feats, near), "dom", k) for k in range(2, doms, 2)]
    inside = (lax.axis_index("rep") == 1) | (lax.axis_index("rep") == 2)
    if count == 4:
        far = swapped(feats, "rep", 3)
        two = relayed(jnp.where(inside, far, feats), -1)
        panels = [feats, far, swapped(feats, "rep", 1), two]
    else:
        panels = [feats] + [swapped(feats, "rep", k) for k in range(count - 1, 0, -1)]
    a = call(
        functools.partial(arrange, count), [shape((rows, count * rows), BF16)],
        (after(after(me, near), even[2]), in_cols.transpose(0, 2, 1), in_vals), "ssh",
        scratch=[pltpu.VMEM(in_vals.shape, BF16), pltpu.SemaphoreType.DMA((blocks,))], name="arrange")[0]
    odd = [near] + [swapped(after(value, a), "dom", 1) for n, value in enumerate(even) if n]
    others = [value for pair in zip(even, odd) for value in pair][1:]
    begun = call(begin, [shape((rows, width), F32)], (a, *panels[:-1]), "v" * count, name="begin")[0]
    activated, keep, give, *terms, grad_agg = call(
        functools.partial(layer, count, doms),
        [flat] + [shape((width // 2, width), BF16)] * 2 + [flat] * (count - 2),
        (me, requests, off_ref, panels[-1], begun, *others, a, off_vals, weight, bias.reshape(1, width), cotangent),
        "sss" + "v" * (doms + 6),
        scratch=[pltpu.VMEM((width, width), F32), pltpu.VMEM((slots, edge, width), BF16)],
        flops=10**9, name="layer")
    part = (keep.astype(F32) + swapped(give, "dom", 1).astype(F32)).astype(BF16)
    first = part
    part = joined(part, "dom", dom_steps[0])
    own, near_terms, next_terms, outer = call(
        spread_rest, [flat, flat, flat, shape((doms, cap * (edge + 16), width), BF16)], (requests, off_ref, a, off_vals, grad_agg), "ssvvv",
        scratch=[pltpu.VMEM((slots, edge, width), F32)], flops=10**9, name="rest")
    terms = dict(zip([k for k in turns(count) if k > 2], terms)) | {2: next_terms}
    got = [swapped(after(terms[k], first if k == 2 else None), "rep", k) for k in range(count - 1, 1, -1)]
    coming, one, grad_weight = fenced(sure, exchange, outer, part, near_terms)
    grad_feats = call(functools.partial(finish, cap, edge), [flat], (coming, own, *got, one), "v" * (count + 1), name="finish")[0]
    return (activated, grad_feats, grad_weight)


def solution(mesh):
    in_specs = (
        P(("rep", "dom"), None),
        P(("rep", "dom"), None),
        P(),
        P(),
        P(("rep", "dom"), None, None, None, None),
        P(("rep", "dom"), None, None),
        P(("rep", "dom"), None, None, None),
        P(("rep", "dom"), None),
        P("rep", "dom", None, None),
    )
    out_specs = (P(("rep", "dom"), None), P(("rep", "dom"), None), P())
    return jax.shard_map(local, mesh=mesh, in_specs=in_specs, out_specs=out_specs, check_vma=False)
```

```python
import functools
import math

import jax
import jax.numpy as jnp
from jax import lax
from jax.experimental import pallas as pl
from jax.experimental.pallas import tpu as pltpu
from jax.sharding import PartitionSpec as P

F32, BF16 = jnp.float32, jnp.bfloat16
ROOT = math.sqrt(2.0 / math.pi)
CUBIC = 0.044715


def turns(count):
    return [0, 3, 1, 2] if count == 4 else [0] + list(range(count - 1, 0, -1))


def swapped(value, axis, k):
    return lax.ppermute(value, axis, [(i, i ^ k) for i in range(lax.axis_size(axis))])


def relayed(value, turns):
    pairs = [(0, 1), (1, 3), (3, 2), (2, 0)]
    return lax.ppermute(value, "rep", [pair[::turns] for pair in pairs])


def after(value, other):
    return value if other is None else lax.optimization_barrier((value, other))[0]


def fenced(sure, body, *args):
    blank = lambda *args: jax.tree.map(lambda s: jnp.zeros(s.shape, s.dtype), jax.eval_shape(body, *args))
    return lax.cond(sure, body, blank, *args)


def call(body, outs, args, kinds, scratch=(), flops=0, name=None):
    spaces = {"s": pltpu.SMEM, "v": pltpu.VMEM, "h": pltpu.HBM}
    nbytes = sum(math.prod(a.shape) * a.dtype.itemsize for a in (*args, *outs))
    work = sum(math.prod(s.shape) * jnp.dtype(s.dtype).itemsize for s in scratch if s.memory_space == pltpu.VMEM)
    return pl.pallas_call(
        body,
        out_shape=outs,
        in_specs=[pl.BlockSpec(memory_space=spaces[k]) for k in kinds],
        out_specs=[pl.BlockSpec(memory_space=pltpu.VMEM) for _ in outs],
        scratch_shapes=list(scratch),
        cost_estimate=pl.CostEstimate(flops=flops, bytes_accessed=nbytes, transcendentals=0),
        compiler_params=pltpu.CompilerParams(vmem_limit_bytes=nbytes + work + (4 << 20)),
        name=name,
    )(*args)


def arrange(count, me_ref, cols_ref, in_hbm, a_ref, in_ref, in_sem):
    blocks, _, pairs, edge, _ = in_ref.shape
    rows = blocks * edge
    copies = [pltpu.make_async_copy(in_hbm.at[b], in_ref.at[b], in_sem.at[b]) for b in range(blocks)]
    for copy in copies:
        copy.start()
    a_ref[...] = jnp.zeros_like(a_ref)
    for b in range(blocks):
        copies[b].wait()
        for n in range(count):
            s = me_ref[0] ^ turns(count)[n]
            for k in range(pairs):
                start = pl.multiple_of(n * rows + cols_ref[b, k, s] * edge, edge)
                a_ref[b * edge:(b + 1) * edge, pl.ds(start, edge)] = in_ref[b, s, k]


def dot(left, right):
    return jnp.dot(left, right, preferred_element_type=F32)


def dot_t(left, right):
    return lax.dot_general(left, right, (((0,), (0,)), ((), ())), preferred_element_type=F32)


def begin(a_ref, *args):
    panels, sum_ref = args[:-1], args[-1]
    rows = sum_ref.shape[0]
    sum_ref[...] = dot(a_ref[:, :len(panels) * rows], jnp.concatenate([ref[...] for ref in panels], axis=0))


def layer(count, doms, me_ref, want_ref, refs_ref, *args):
    last_ref, sum_ref, others = args[0], args[1], args[2:doms + 1]
    (a_ref, off_ref, weight_ref, bias_ref, cot_ref,
     act_ref, keep_ref, give_ref, *rest) = args[doms + 1:]
    outs, (grad_ref, term_ref, block_ref) = rest[:-3], rest[-3:]
    blocks, tiles, edge, _ = off_ref.shape
    rows, cap = blocks * edge, want_ref.shape[0]
    for n in range(1, doms):
        f = me_ref[1] ^ n
        for c in range(cap):
            block_ref[f * cap + c] = others[n - 1][pl.ds(pl.multiple_of(want_ref[c, f] * edge, edge), edge), :]
    inner = sum_ref[...] + dot(a_ref[:, (count - 1) * rows:], last_ref[...])
    sums = []
    for b in range(blocks):
        left = jnp.concatenate([off_ref[b, k] for k in range(tiles)], axis=1)
        right = jnp.concatenate([block_ref[refs_ref[b, k]] for k in range(tiles)], axis=0)
        sums.append(inner[b * edge:(b + 1) * edge] + dot(left, right))
    agg = jnp.concatenate(sums, axis=0).astype(BF16)
    v = dot(agg, weight_ref[...]) + bias_ref[...]
    t = jnp.tanh(ROOT * (v + CUBIC * (v * v * v)))
    act_ref[...] = (0.5 * v * (1.0 + t)).astype(BF16)
    slope = 0.5 * (1.0 + t) + 0.5 * v * (1.0 - t * t) * (ROOT * (1.0 + 3.0 * CUBIC * (v * v)))
    grad_pre = (cot_ref[...].astype(F32) * slope).astype(BF16)
    grad_agg = lax.dot_general(
        grad_pre, weight_ref[...], (((1,), (1,)), ((), ())), preferred_element_type=F32).astype(BF16)
    grad_ref[...] = grad_agg
    for out, n in zip(outs, [n for n, k in enumerate(turns(count)) if k > 2]):
        out[...] = dot_t(a_ref[:, n * rows:(n + 1) * rows], grad_agg).astype(BF16)
    term_ref[...] = dot_t(agg, grad_pre)
    half, core = keep_ref.shape[0], me_ref[1] & 1
    keep_ref[...] = term_ref[pl.ds(pl.multiple_of(core * half, half), half), :].astype(BF16)
    give_ref[...] = term_ref[pl.ds(pl.multiple_of((1 - core) * half, half), half), :].astype(BF16)


def spread_rest(want_ref, refs_ref, a_ref, off_ref, grad_ref, made_ref, act_ref, own_ref, near_ref, next_ref, out_ref, total_ref):
    blocks, tiles, edge, _ = off_ref.shape
    cap, doms = want_ref.shape
    act_ref[...] = made_ref[...]
    grad_agg = grad_ref[...]
    rows = grad_agg.shape[0]
    order = turns(a_ref.shape[1] // rows)
    for ref, n in ((own_ref, order.index(0)), (near_ref, order.index(1)), (next_ref, order.index(2))):
        ref[...] = dot_t(a_ref[:, n * rows:(n + 1) * rows], grad_agg).astype(BF16)
    total_ref[...] = jnp.zeros_like(total_ref)
    for b in range(blocks):
        grad_b = grad_agg[b * edge:(b + 1) * edge]
        for k in range(tiles):
            total_ref[refs_ref[b, k]] += dot_t(off_ref[b, k], grad_b)
    for f in range(doms):
        for c in range(cap):
            out_ref[f, c * edge:(c + 1) * edge, :] = total_ref[f * cap + c].astype(BF16)
            top = cap * edge + c * 16
            out_ref[f, top:top + 16, :] = jnp.full((16, out_ref.shape[2]), want_ref[c, f], jnp.int32).astype(BF16)


def joined(part, axis, k):
    return (part.astype(F32) + swapped(part, axis, k).astype(F32)).astype(BF16)


def join(scale, me_ref, part_ref, other_ref, out_ref):
    half, core = part_ref.shape[0], me_ref[1] & 1
    out_ref[pl.ds(pl.multiple_of(core * half, half), half), :] = (part_ref[...].astype(F32) * scale).astype(BF16)
    out_ref[pl.ds(pl.multiple_of((1 - core) * half, half), half), :] = (other_ref[...].astype(F32) * scale).astype(BF16)


def finish(cap, edge, coming_ref, *args):
    terms, out_ref = args[:-1], args[-1]
    for j in range(out_ref.shape[0] // edge):
        part = slice(j * edge, (j + 1) * edge)
        total = terms[0][part, :].astype(F32)
        for ref in terms[1:]:
            total += ref[part, :].astype(F32)
        for f in range(coming_ref.shape[0]):
            for c in range(cap):
                top = cap * edge + c * 16
                place = coming_ref[f, top:top + 1, :].astype(F32)
                total += jnp.where(place == j, coming_ref[f, c * edge:(c + 1) * edge, :].astype(F32), 0.0)
        out_ref[part, :] = total.astype(BF16)


def local(feats, cotangent, weight, bias, in_vals, in_cols, off_vals, off_ref, want):
    count, doms = lax.axis_size("rep"), lax.axis_size("dom")
    me = jnp.stack([lax.axis_index("rep"), lax.axis_index("dom")]).astype(jnp.int32)
    blocks, _, _, edge, _ = in_vals.shape
    rows, width = feats.shape
    requests = want.transpose(0, 1, 3, 2).reshape(want.shape[3], want.shape[2])
    cap = requests.shape[0]
    shape = jax.ShapeDtypeStruct
    flat = shape((rows, width), BF16)

    slots = doms * cap
    sure = requests[0, 0] >= 0
    scale = 1.0 / math.sqrt(rows * count * doms)

    dom_steps = [k for k in (4, 2) if k < doms] + [1 << n for n in range(3, doms.bit_length() - 1)]

    def exchange(outer, part, one):
        one = swapped(one, "rep", 1)
        coming = lax.all_to_all(outer, "dom", split_axis=0, concat_axis=0, tiled=True)
        for axis, steps in (("dom", dom_steps[1:]), ("rep", [1 << n for n in range(count.bit_length() - 1)])):
            for k in steps:
                part = joined(part, axis, k)
        return coming, one, call(functools.partial(join, scale), [shape((width, width), BF16)], (me, part, swapped(part, "dom", 1)), "svv", name="join")[0]

    near = swapped(feats, "dom", 1)
    even = [feats] + [swapped(feats if k == 4 else after(feats, near), "dom", k) for k in range(2, doms, 2)]
    inside = (lax.axis_index("rep") == 1) | (lax.axis_index("rep") == 2)
    if count == 4:
        far = swapped(feats, "rep", 3)
        two = relayed(jnp.where(inside, far, feats), -1)
        panels = [feats, far, swapped(feats, "rep", 1), two]
    else:
        panels = [feats] + [swapped(feats, "rep", k) for k in range(count - 1, 0, -1)]
    a = call(
        functools.partial(arrange, count), [shape((rows, count * rows), BF16)],
        (after(after(me, near), even[2]), in_cols.transpose(0, 2, 1), in_vals), "ssh",
        scratch=[pltpu.VMEM(in_vals.shape, BF16), pltpu.SemaphoreType.DMA((blocks,))], name="arrange")[0]
    odd = [near] + [swapped(after(value, a), "dom", 1) for n, value in enumerate(even) if n]
    others = [value for pair in zip(even, odd) for value in pair][1:]
    begun = call(begin, [shape((rows, width), F32)], (a, *panels[:-1]), "v" * count, name="begin")[0]
    made, keep, give, *terms, grad_agg = call(
        functools.partial(layer, count, doms),
        [flat] + [shape((width // 2, width), BF16)] * 2 + [flat] * (count - 2),
        (me, requests, off_ref, panels[-1], begun, *others, a, off_vals, weight, bias.reshape(1, width), cotangent),
        "sss" + "v" * (doms + 6),
        scratch=[pltpu.VMEM((width, width), F32), pltpu.VMEM((slots, edge, width), BF16)],
        flops=10**9, name="layer")
    part = (keep.astype(F32) + swapped(give, "dom", 1).astype(F32)).astype(BF16)
    first = part
    part = joined(part, "dom", dom_steps[0])
    activated, own, near_terms, next_terms, outer = call(
        spread_rest, [flat, flat, flat, flat, shape((doms, cap * (edge + 16), width), BF16)], (requests, off_ref, a, off_vals, grad_agg, made), "ssvvvv",
        scratch=[pltpu.VMEM((slots, edge, width), F32)], flops=10**9, name="rest")
    terms = dict(zip([k for k in turns(count) if k > 2], terms)) | {2: next_terms}
    got = [swapped(after(terms[k], first if k == 2 else None), "rep", k) for k in range(count - 1, 1, -1)]
    coming, one, grad_weight = fenced(sure, exchange, outer, part, near_terms)
    grad_feats = call(functools.partial(finish, cap, edge), [flat], (coming, own, *got, one), "v" * (count + 1), name="finish")[0]
    return (activated, grad_feats, grad_weight)


def solution(mesh):
    in_specs = (
        P(("rep", "dom"), None),
        P(("rep", "dom"), None),
        P(),
        P(),
        P(("rep", "dom"), None, None, None, None),
        P(("rep", "dom"), None, None),
        P(("rep", "dom"), None, None, None),
        P(("rep", "dom"), None),
        P("rep", "dom", None, None),
    )
    out_specs = (P(("rep", "dom"), None), P(("rep", "dom"), None), P())
    return jax.shard_map(local, mesh=mesh, in_specs=in_specs, out_specs=out_specs, check_vma=False)
```

```python
import functools
import math

import jax
import jax.numpy as jnp
from jax import lax
from jax.experimental import pallas as pl
from jax.experimental.pallas import tpu as pltpu
from jax.sharding import PartitionSpec as P

F32, BF16 = jnp.float32, jnp.bfloat16
ROOT = math.sqrt(2.0 / math.pi)
CUBIC = 0.044715


def turns(count):
    return [0, 3, 1, 2] if count == 4 else [0] + list(range(count - 1, 0, -1))


def swapped(value, axis, k):
    return lax.ppermute(value, axis, [(i, i ^ k) for i in range(lax.axis_size(axis))])


def relayed(value, turns):
    pairs = [(0, 1), (1, 3), (3, 2), (2, 0)]
    return lax.ppermute(value, "rep", [pair[::turns] for pair in pairs])


def after(value, other):
    return value if other is None else lax.optimization_barrier((value, other))[0]


def fenced(sure, body, *args):
    blank = lambda *args: jax.tree.map(lambda s: jnp.zeros(s.shape, s.dtype), jax.eval_shape(body, *args))
    return lax.cond(sure, body, blank, *args)


def call(body, outs, args, kinds, scratch=(), flops=0, name=None):
    spaces = {"s": pltpu.SMEM, "v": pltpu.VMEM, "h": pltpu.HBM}
    nbytes = sum(math.prod(a.shape) * a.dtype.itemsize for a in (*args, *outs))
    work = sum(math.prod(s.shape) * jnp.dtype(s.dtype).itemsize for s in scratch if s.memory_space == pltpu.VMEM)
    return pl.pallas_call(
        body,
        out_shape=outs,
        in_specs=[pl.BlockSpec(memory_space=spaces[k]) for k in kinds],
        out_specs=[pl.BlockSpec(memory_space=pltpu.VMEM) for _ in outs],
        scratch_shapes=list(scratch),
        cost_estimate=pl.CostEstimate(flops=flops, bytes_accessed=nbytes, transcendentals=0),
        compiler_params=pltpu.CompilerParams(vmem_limit_bytes=nbytes + work + (4 << 20)),
        name=name,
    )(*args)


def arrange(count, me_ref, cols_ref, in_hbm, a_ref, in_ref, in_sem):
    blocks, _, pairs, edge, _ = in_ref.shape
    rows = blocks * edge
    copies = [pltpu.make_async_copy(in_hbm.at[b], in_ref.at[b], in_sem.at[b]) for b in range(blocks)]
    for copy in copies:
        copy.start()
    a_ref[...] = jnp.zeros_like(a_ref)
    for b in range(blocks):
        copies[b].wait()
        for n in range(count):
            s = me_ref[0] ^ turns(count)[n]
            for k in range(pairs):
                start = pl.multiple_of(n * rows + cols_ref[b, k, s] * edge, edge)
                a_ref[b * edge:(b + 1) * edge, pl.ds(start, edge)] = in_ref[b, s, k]


def dot(left, right):
    return jnp.dot(left, right, preferred_element_type=F32)


def dot_t(left, right):
    return lax.dot_general(left, right, (((0,), (0,)), ((), ())), preferred_element_type=F32)


def begin(a_ref, *args):
    panels, sum_ref = args[:-1], args[-1]
    rows = sum_ref.shape[0]
    sum_ref[...] = dot(a_ref[:, :len(panels) * rows], jnp.concatenate([ref[...] for ref in panels], axis=0))


def layer(count, doms, me_ref, want_ref, refs_ref, *args):
    last_ref, sum_ref, others = args[0], args[1], args[2:doms + 1]
    (a_ref, off_ref, weight_ref, bias_ref, cot_ref,
     act_ref, keep_ref, give_ref, *rest) = args[doms + 1:]
    outs, (grad_ref, term_ref, block_ref) = rest[:-3], rest[-3:]
    blocks, tiles, edge, _ = off_ref.shape
    rows, cap = blocks * edge, want_ref.shape[0]
    for n in range(1, doms):
        f = me_ref[1] ^ n
        for c in range(cap):
            block_ref[f * cap + c] = others[n - 1][pl.ds(pl.multiple_of(want_ref[c, f] * edge, edge), edge), :]
    inner = sum_ref[...] + dot(a_ref[:, (count - 1) * rows:], last_ref[...])
    sums = []
    for b in range(blocks):
        left = jnp.concatenate([off_ref[b, k] for k in range(tiles)], axis=1)
        right = jnp.concatenate([block_ref[refs_ref[b, k]] for k in range(tiles)], axis=0)
        sums.append(inner[b * edge:(b + 1) * edge] + dot(left, right))
    agg = jnp.concatenate(sums, axis=0).astype(BF16)
    v = dot(agg, weight_ref[...]) + bias_ref[...]
    t = jnp.tanh(ROOT * (v + CUBIC * (v * v * v)))
    act_ref[...] = (0.5 * v * (1.0 + t)).astype(BF16)
    slope = 0.5 * (1.0 + t) + 0.5 * v * (1.0 - t * t) * (ROOT * (1.0 + 3.0 * CUBIC * (v * v)))
    grad_pre = (cot_ref[...].astype(F32) * slope).astype(BF16)
    grad_agg = lax.dot_general(
        grad_pre, weight_ref[...], (((1,), (1,)), ((), ())), preferred_element_type=F32).astype(BF16)
    grad_ref[...] = grad_agg
    for out, n in zip(outs, [n for n, k in enumerate(turns(count)) if k > 2]):
        out[...] = dot_t(a_ref[:, n * rows:(n + 1) * rows], grad_agg).astype(BF16)
    term_ref[...] = dot_t(agg, grad_pre)
    half, core = keep_ref.shape[0], me_ref[1] & 1
    keep_ref[...] = term_ref[pl.ds(pl.multiple_of(core * half, half), half), :].astype(BF16)
    give_ref[...] = term_ref[pl.ds(pl.multiple_of((1 - core) * half, half), half), :].astype(BF16)


def spread_rest(want_ref, refs_ref, a_ref, off_ref, grad_ref, made_ref, act_ref, own_ref, near_ref, next_ref, out_ref, total_ref):
    blocks, tiles, edge, _ = off_ref.shape
    cap, doms = want_ref.shape
    act_ref[...] = made_ref[...]
    grad_agg = grad_ref[...]
    rows = grad_agg.shape[0]
    order = turns(a_ref.shape[1] // rows)
    for ref, n in ((own_ref, order.index(0)), (near_ref, order.index(1)), (next_ref, order.index(2))):
        ref[...] = dot_t(a_ref[:, n * rows:(n + 1) * rows], grad_agg).astype(BF16)
    total_ref[...] = jnp.zeros_like(total_ref)
    for b in range(blocks):
        grad_b = grad_agg[b * edge:(b + 1) * edge]
        for k in range(tiles):
            total_ref[refs_ref[b, k]] += dot_t(off_ref[b, k], grad_b)
    for f in range(doms):
        for c in range(cap):
            out_ref[f, c * edge:(c + 1) * edge, :] = total_ref[f * cap + c].astype(BF16)
            top = cap * edge + c * 16
            out_ref[f, top:top + 16, :] = jnp.full((16, out_ref.shape[2]), want_ref[c, f], jnp.int32).astype(BF16)


def joined(part, axis, k):
    return (part.astype(F32) + swapped(part, axis, k).astype(F32)).astype(BF16)


def join(scale, me_ref, part_ref, other_ref, out_ref):
    half, core = part_ref.shape[0], me_ref[1] & 1
    out_ref[pl.ds(pl.multiple_of(core * half, half), half), :] = (part_ref[...].astype(F32) * scale).astype(BF16)
    out_ref[pl.ds(pl.multiple_of((1 - core) * half, half), half), :] = (other_ref[...].astype(F32) * scale).astype(BF16)


def finish(cap, edge, coming_ref, *args):
    terms, (out_ref, total_ref) = args[:-2], args[-2:]
    total = terms[0][...].astype(F32)
    for ref in terms[1:]:
        total += ref[...].astype(F32)
    total_ref[...] = total
    for f in range(coming_ref.shape[0]):
        for c in range(cap):
            top = cap * edge + c * 16
            place = coming_ref[f, top:top + 1, :].astype(F32)
            block = coming_ref[f, c * edge:(c + 1) * edge, :].astype(F32)
            for j in range(out_ref.shape[0] // edge):
                total_ref[j * edge:(j + 1) * edge, :] += jnp.where(place == j, block, 0.0)
    out_ref[...] = total_ref[...].astype(BF16)


def local(feats, cotangent, weight, bias, in_vals, in_cols, off_vals, off_ref, want):
    count, doms = lax.axis_size("rep"), lax.axis_size("dom")
    me = jnp.stack([lax.axis_index("rep"), lax.axis_index("dom")]).astype(jnp.int32)
    blocks, _, _, edge, _ = in_vals.shape
    rows, width = feats.shape
    requests = want.transpose(0, 1, 3, 2).reshape(want.shape[3], want.shape[2])
    cap = requests.shape[0]
    shape = jax.ShapeDtypeStruct
    flat = shape((rows, width), BF16)

    slots = doms * cap
    sure = requests[0, 0] >= 0
    scale = 1.0 / math.sqrt(rows * count * doms)

    dom_steps = [k for k in (4, 2) if k < doms] + [1 << n for n in range(3, doms.bit_length() - 1)]

    def exchange(outer, part, one):
        one = swapped(one, "rep", 1)
        coming = lax.all_to_all(outer, "dom", split_axis=0, concat_axis=0, tiled=True)
        for axis, steps in (("dom", dom_steps[1:]), ("rep", [1 << n for n in range(count.bit_length() - 1)])):
            for k in steps:
                part = joined(part, axis, k)
        return coming, one, call(functools.partial(join, scale), [shape((width, width), BF16)], (me, part, swapped(part, "dom", 1)), "svv", name="join")[0]

    near = swapped(feats, "dom", 1)
    even = [feats] + [swapped(feats if k == 4 else after(feats, near), "dom", k) for k in range(2, doms, 2)]
    inside = (lax.axis_index("rep") == 1) | (lax.axis_index("rep") == 2)
    if count == 4:
        far = swapped(feats, "rep", 3)
        two = relayed(jnp.where(inside, far, feats), -1)
        panels = [feats, far, swapped(feats, "rep", 1), two]
    else:
        panels = [feats] + [swapped(feats, "rep", k) for k in range(count - 1, 0, -1)]
    a = call(
        functools.partial(arrange, count), [shape((rows, count * rows), BF16)],
        (after(after(me, near), even[2]), in_cols.transpose(0, 2, 1), in_vals), "ssh",
        scratch=[pltpu.VMEM(in_vals.shape, BF16), pltpu.SemaphoreType.DMA((blocks,))], name="arrange")[0]
    odd = [near] + [swapped(after(value, a), "dom", 1) for n, value in enumerate(even) if n]
    others = [value for pair in zip(even, odd) for value in pair][1:]
    begun = call(begin, [shape((rows, width), F32)], (a, *panels[:-1]), "v" * count, name="begin")[0]
    made, keep, give, *terms, grad_agg = call(
        functools.partial(layer, count, doms),
        [flat] + [shape((width // 2, width), BF16)] * 2 + [flat] * (count - 2),
        (me, requests, off_ref, panels[-1], begun, *others, a, off_vals, weight, bias.reshape(1, width), cotangent),
        "sss" + "v" * (doms + 6),
        scratch=[pltpu.VMEM((width, width), F32), pltpu.VMEM((slots, edge, width), BF16)],
        flops=10**9, name="layer")
    part = (keep.astype(F32) + swapped(give, "dom", 1).astype(F32)).astype(BF16)
    first = part
    part = joined(part, "dom", dom_steps[0])
    activated, own, near_terms, next_terms, outer = call(
        spread_rest, [flat, flat, flat, flat, shape((doms, cap * (edge + 16), width), BF16)], (requests, off_ref, a, off_vals, grad_agg, made), "ssvvvv",
        scratch=[pltpu.VMEM((slots, edge, width), F32)], flops=10**9, name="rest")
    terms = dict(zip([k for k in turns(count) if k > 2], terms)) | {2: next_terms}
    got = [swapped(after(terms[k], first if k == 2 else None), "rep", k) for k in range(count - 1, 1, -1)]
    coming, one, grad_weight = fenced(sure, exchange, outer, part, near_terms)
    grad_feats = call(functools.partial(finish, cap, edge), [flat], (coming, own, *got, one), "v" * (count + 1),
        scratch=[pltpu.VMEM((rows, width), F32)], name="finish")[0]
    return (activated, grad_feats, grad_weight)


def solution(mesh):
    in_specs = (
        P(("rep", "dom"), None),
        P(("rep", "dom"), None),
        P(),
        P(),
        P(("rep", "dom"), None, None, None, None),
        P(("rep", "dom"), None, None),
        P(("rep", "dom"), None, None, None),
        P(("rep", "dom"), None),
        P("rep", "dom", None, None),
    )
    out_specs = (P(("rep", "dom"), None), P(("rep", "dom"), None), P())
    return jax.shard_map(local, mesh=mesh, in_specs=in_specs, out_specs=out_specs, check_vma=False)
```
